512 devices in a mesh: slab: 512 (over x, z, y, core).
Axes of the slice: x: 4, y: 4, z: 16, core: 2. Of those that a mesh axis runs over, the one named last changes fastest.
Arguments:
- load: float32 [3, 1048576], P(None, 'slab'), may hold values from -6 to 6
- element_mats: bfloat16 [12, 12, 1048576], P(None, None, 'slab'), as said below
- connect: int32 [4, 1048576], P(None, 'slab'), may hold values from 0 to 2047, as said below
- shared: int32 [2, 131072], P(None, 'slab'), may hold values from 0 to 2047, as said below
Outputs:
- accel: float32 [3, 1048576], P(None, 'slab')
- residual: float32 [3, 1048576], P(None, 'slab')
The draws below stay inside these ranges and needn't reach their ends.
Inputs may be any that keep to these rules, and one draw needn't show every extreme that they name: `connect`: slab-local node numbers; the four nodes of an element differ, and every node of a slab belongs to some element of that slab. `shared`: within a slab the 256 numbers of row 0 and of row 1 are all distinct; entry j of a slab's row 1 and entry j of the next slab's row 0 are the same physical node. `element_mats`: each element's matrix is symmetric with a strictly dominant positive diagonal.
All inputs are finite; a program needn't handle non-finite values.
Results may differ from the reference program's by a relative error of at most 0.0003.
Values sent between devices are 32-bit elements; how exact they have to be, the bound alone decides.
No kernel may reach another device: no remote copies, remote signals or barrier semaphores. Data moves between devices by JAX's collectives and lax.ppermute only.
A program may use at most 64 MiB of HBM per device.

```python
import jax
import jax.numpy as jnp
from jax import lax

E_DEV = 2048
SHARED = 256
ITERS = 4
ELEMS = 1048576
NODES = 1048576


def draw_element_mats(key, part):
    key = jax.random.fold_in(key, 11)
    key_off, key_mass, key_scale = jax.random.split(key, 3)
    offdiag = jax.random.uniform(key_off, (12, 12, ELEMS), jnp.float32, -1.0, 1.0)
    symmetric = 0.5 * (offdiag + offdiag.transpose(1, 0, 2))
    mass = jnp.exp(jax.random.uniform(key_mass, (ELEMS,), jnp.float32, jnp.log(0.2), jnp.log(2.0)))
    identity = jnp.eye(12, dtype=jnp.float32)[:, :, None]
    matrix = symmetric * (1.0 - identity) + identity * (11.0 + mass)
    scale = jnp.exp(jax.random.uniform(key_scale, (ELEMS,), jnp.float32, jnp.log(0.5), jnp.log(2.0)))
    return (matrix * scale).astype(jnp.bfloat16)


def connect_slab(key):
    key_base, key_one, key_two, key_three = jax.random.split(key, 4)
    base = jax.random.permutation(key_base, E_DEV).astype(jnp.int32)
    first = jax.random.randint(key_one, (E_DEV,), 1, 22, jnp.int32)
    second = first + jax.random.randint(key_two, (E_DEV,), 1, 22, jnp.int32)
    third = second + jax.random.randint(key_three, (E_DEV,), 1, 22, jnp.int32)
    offsets = jnp.stack([jnp.zeros_like(first), first, second, third])
    return (base[None, :] + offsets) % E_DEV


def draw_connect(key, part):
    key = jax.random.fold_in(key, 23)
    slabs = ELEMS // E_DEV
    keys = jax.random.split(key, slabs)
    blocks = jax.vmap(connect_slab)(keys)
    return blocks.transpose(1, 0, 2).reshape(4, ELEMS).astype(jnp.int32)


def shared_slab(key):
    order = jax.random.permutation(key, E_DEV).astype(jnp.int32)
    return order[:2 * SHARED].reshape(2, SHARED)


def draw_shared(key, part):
    key = jax.random.fold_in(key, 37)
    slabs = ELEMS // E_DEV
    keys = jax.random.split(key, slabs)
    lists = jax.vmap(shared_slab)(keys)
    return lists.transpose(1, 0, 2).reshape(2, slabs * SHARED).astype(jnp.int32)


def block_scale(key, shape, cuts, least, largest):
    factor_of, own = 1.0, jax.random.fold_in(key, 6)
    for position, blocks in cuts:
        heights = jnp.exp(jax.random.uniform(jax.random.fold_in(own, position), (blocks,), jnp.float32, least / len(cuts), largest / len(cuts)))
        factor_of = factor_of * jnp.repeat(heights, shape[position] // blocks).reshape([-1 if axis == position else 1 for axis in range(len(shape))])
    return factor_of


def centred(key, dims, spread, reach, cuts=(), kind=jnp.bfloat16):
    values = spread * jax.random.normal(key, dims, jnp.float32)
    if cuts:
        values = values * block_scale(key, dims, cuts, -0.22, 0.18)
    return jnp.clip(values, -reach, reach).astype(kind)


def setup_inputs(seed: int = 0) -> dict:
    streams_of = jax.random.split(jax.random.key(seed), 5)
    return {
        "load": centred(streams_of[0], (3, NODES), 1.0, 6.0, ((1, 512),), jnp.float32),
        "element_mats": draw_element_mats(jax.random.fold_in(streams_of[4], 71), 0),
        "connect": draw_connect(jax.random.fold_in(streams_of[4], 71), 0),
        "shared": draw_shared(jax.random.fold_in(streams_of[4], 71), 0),
    }


def element_apply(kblock, conn, field):
    gathered = field[:, conn]
    gathered = gathered.transpose(1, 0, 2).reshape(12, -1)
    result = kblock[:, 0, :].astype(jnp.float32) * gathered[0]
    for column in range(1, 12):
        result = result + kblock[:, column, :].astype(jnp.float32) * gathered[column]
    values = result.reshape(4, 3, -1).transpose(1, 0, 2).reshape(3, -1)
    return jnp.zeros(field.shape, jnp.float32).at[:, conn.reshape(-1)].add(values)


def diag_partial(kblock, conn, node_count):
    entries = jnp.stack([kblock[i, i, :].astype(jnp.float32) for i in range(12)])
    values = entries.reshape(4, 3, -1).transpose(1, 0, 2).reshape(3, -1)
    return jnp.zeros((3, node_count), jnp.float32).at[:, conn.reshape(-1)].add(values)


def per_slab(array, slabs):
    chans = array.shape[0]
    return array.reshape(chans, slabs, -1).transpose(1, 0, 2)


def assemble_all(partial_value, lists):
    left_vals = jax.vmap(lambda p, l: p[:, l[0]])(partial_value, lists)
    right_vals = jax.vmap(lambda p, l: p[:, l[1]])(partial_value, lists)
    from_left = jnp.concatenate([jnp.zeros_like(right_vals[:1]), right_vals[:-1]], axis=0)
    from_right = jnp.concatenate([left_vals[1:], jnp.zeros_like(left_vals[:1])], axis=0)
    return jax.vmap(lambda p, l, a, b: p.at[:, l[0]].add(a).at[:, l[1]].add(b))(partial_value, lists, from_left, from_right)


def reference(load, element_mats, connect, shared):
    slabs = ELEMS // E_DEV
    lists = per_slab(shared, slabs)
    index_all = jnp.arange(slabs, dtype=jnp.int32)

    def apply_all(field_all):
        def one(slab_id):
            kblock = lax.dynamic_slice_in_dim(element_mats, slab_id * E_DEV, E_DEV, 2)
            conn = lax.dynamic_slice_in_dim(connect, slab_id * E_DEV, E_DEV, 1)
            return element_apply(kblock, conn, field_all[slab_id])
        return lax.map(one, index_all)

    def diag_one(slab_id):
        kblock = lax.dynamic_slice_in_dim(element_mats, slab_id * E_DEV, E_DEV, 2)
        conn = lax.dynamic_slice_in_dim(connect, slab_id * E_DEV, E_DEV, 1)
        return diag_partial(kblock, conn, E_DEV)

    left_weight = jnp.where(index_all > 0, jnp.float32(0.5), jnp.float32(1.0))
    right_weight = jnp.where(index_all < slabs - 1, jnp.float32(0.5), jnp.float32(1.0))
    weights = jax.vmap(lambda l, a, b: jnp.ones((E_DEV,), jnp.float32).at[l[0]].set(a).at[l[1]].set(b))(lists, left_weight, right_weight)

    def inner(first, second):
        return jnp.sum(weights * jnp.sum(first * second, axis=1))

    lumped = lax.map(diag_one, index_all)
    both = assemble_all(jnp.concatenate([per_slab(load, slabs), lumped], axis=1), lists)
    force = both[:, :3]
    diagonal = both[:, 3:]
    accel = jnp.zeros_like(force)
    residual = force
    precond = residual / diagonal
    direction = precond
    gamma = inner(residual, precond)
    for step in range(ITERS):
        image = assemble_all(apply_all(direction), lists)
        alpha = gamma / inner(direction, image)
        accel = accel + alpha * direction
        residual = residual - alpha * image
        precond = residual / diagonal
        gamma_next = inner(residual, precond)
        direction = precond + (gamma_next / gamma) * direction
        gamma = gamma_next
    accel_out = accel.transpose(1, 0, 2).reshape(3, -1)
    residual_out = residual.transpose(1, 0, 2).reshape(3, -1)
    return accel_out, residual_out
```

```python
import jax
import jax.numpy as jnp
from jax import lax
from jax.experimental import pallas as pl
from jax.experimental.pallas import tpu as pltpu
from jax.sharding import Mesh, PartitionSpec as P

ITERS = 4
AXES = ("x", "z", "y", "c")
GROUP = ("x", "y", "c")
NODES = 2048
ELEMS = 2048
SHARED = 256
SPLITS = 3
PIVOT_FLOOR = 1e-3
F32 = jnp.float32
BF16 = jnp.bfloat16
VMEM_LIMIT = 32 * 1024 * 1024


def iota(shape, dim):
    return lax.broadcasted_iota(jnp.int32, shape, dim)


def lane_take(table, lanes):
    return jnp.take_along_axis(table, lanes, axis=1, mode="promise_in_bounds")


def pick(parts, high):
    bit = 0
    while len(parts) > 1:
        odd = (high & (1 << bit)) != 0
        parts = [jnp.where(odd, parts[i + 1], parts[i]) for i in range(0, len(parts), 2)]
        bit += 1
    return parts[0]


def field_rows(field, block):
    high, half = block >> 1, block & 1
    return [
        jnp.broadcast_to(field[c * 8 + high : c * 8 + high + 1, half * 128 : half * 128 + 128], (8, 128))
        for c in range(3)
    ]


def by_component(rows, comp):
    return jnp.where(comp == 0, rows[0], jnp.where(comp == 1, rows[1], rows[2]))


def halos_of(field, lists):
    comp = iota((8, 128), 0) // 2
    tables = [by_component(field_rows(field, block), comp) for block in range(16)]
    out = []
    for nodes in lists:
        out.append(pick([lane_take(t, nodes & 127) for t in tables], nodes >> 7))
    return out


def assembled(field, inverse, near):
    columns = []
    for half in range(2):
        where_from = inverse[:, half * 128 : half * 128 + 128]
        lanes, code = where_from & 127, where_from >> 7
        rows = []
        for c in range(3):
            tile = field[c * 8 : c * 8 + 8, half * 128 : half * 128 + 128]
            parts = []
            for t in range(4):
                row = 2 * c + (t & 1)
                table = jnp.broadcast_to(near[t >> 1][row : row + 1, :], (8, 128))
                parts.append(lane_take(table, lanes))
            gain = pick(parts, code)
            rows.append(tile + jnp.where(code < 0, 0.0, gain))
        columns.append(jnp.concatenate(rows, axis=0))
    return jnp.concatenate(columns, axis=1)


def corner_lhs(values, conn, comps):
    width = values.shape[1]
    sub = iota((8, width), 0)
    parts = []
    rest = values
    for _ in range(SPLITS - 1):
        top = rest.astype(BF16).astype(F32)
        parts.append(top)
        rest = rest - top
    parts.append(rest)
    out = []
    for n in range(4):
        mask = jnp.broadcast_to(conn[n : n + 1, :] >> 8, (8, width)) == sub
        tiles = []
        for part in parts:
            for c in range(comps):
                row = n * comps + c
                tiles.append(jnp.where(mask, jnp.broadcast_to(part[row : row + 1, :], (8, width)), 0.0))
        if len(tiles) % 2:
            tiles.append(jnp.zeros((8, width), F32))
        out.append(jnp.concatenate(tiles, axis=0).astype(BF16))
    return out


def one_hot(nodes):
    width = nodes.shape[1]
    low = jnp.broadcast_to((nodes & 255).astype(F32), (256, width)).astype(BF16)
    rows = iota((256, width), 0).astype(F32).astype(BF16)
    return jnp.where(rows == low, jnp.ones((), BF16), jnp.zeros((), BF16))


def times_one_hot(lhs, nodes):
    return lax.dot_general(lhs, one_hot(nodes), (((1,), (1,)), ((), ())), preferred_element_type=F32)


def fold_splits(total):
    out = total[0:24]
    for s in range(1, SPLITS):
        out = out + total[24 * s : 24 * s + 24]
    return out


def scatter(values_of, conn_ref):
    total = None
    for block in range(ELEMS // 256):
        start = block * 256
        conn = conn_ref[:, start : start + 256]
        lhs = corner_lhs(values_of(start), conn, 3)
        for n in range(4):
            piece = times_one_hot(lhs[n], conn[n : n + 1, :])
            total = piece if total is None else total + piece
    return fold_splits(total)


def first_kernel(load_ref, mats_ref, conn_ref, shared_ref, load_out, lumped_out, index_out, inverse_out, lists_out, a_out, b_out):
    odd = lax.axis_index("c") == 1
    own = shared_ref[...]
    row0, row1 = own[0:1, :], own[1:2, :]
    side_a = jnp.where(odd, row0, row1)
    side_b = jnp.where(odd, row1, row0)

    sub8 = iota((8, 128), 0)
    lists = []
    for side in (side_a, side_b):
        first = jnp.broadcast_to(side[:, 0:128], (8, 128))
        second = jnp.broadcast_to(side[:, 128:256], (8, 128))
        lists.append(jnp.where((sub8 & 1) == 0, first, second))
    lists_out[0:8, :] = lists[0]
    lists_out[8:16, :] = lists[1]

    sub = iota((8, 256), 0)
    lane = iota((8, 256), 1)
    found = None
    for t, side in enumerate((side_a, side_b)):
        mask = jnp.broadcast_to(side >> 8, (8, 256)) == sub
        place = jnp.where(mask, (lane & 127).astype(F32), 0.0)
        code = jnp.where(mask, (2 * t + (lane >> 7) + 1).astype(F32), 0.0)
        piece = times_one_hot(jnp.concatenate([place, code], axis=0).astype(BF16), side)
        found = piece if found is None else found + piece
    inverse_out[...] = (found[8:16].astype(jnp.int32) - 1) * 128 + found[0:8].astype(jnp.int32)

    for c in range(3):
        for h in range(8):
            load_out[c * 8 + h : c * 8 + h + 1, :] = load_ref[c : c + 1, h * 256 : h * 256 + 256]

    for j in range(12):
        index_out[j : j + 1, :] = conn_ref[j // 3 : j // 3 + 1, :]
    index_out[12:16, :] = jnp.zeros((4, ELEMS), jnp.int32)

    row12 = iota((12, 256), 0)

    def diagonal_of(start):
        out = jnp.zeros((12, 256), F32)
        for j in range(12):
            out = jnp.where(row12 == j, mats_ref[j, :, start : start + 256].astype(F32), out)
        return out

    lumped = scatter(diagonal_of, conn_ref)
    lumped_out[...] = lumped
    load_a, load_b = halos_of(load_out[...], lists)
    lump_a, lump_b = halos_of(lumped, lists)
    a_out[0:8, :] = load_a
    a_out[8:16, :] = lump_a
    b_out[0:8, :] = load_b
    b_out[8:16, :] = lump_b


def apply_off_diagonal(field, mats_ref, conn_ref, index_ref, table_ref):
    sub = iota((8, 128), 0)
    for block in range(16):
        rows = field_rows(field, block)
        table_ref[block, 0:8, :] = by_component(rows, sub % 3)
        table_ref[block, 8:16, :] = by_component(rows, (sub + 2) % 3)
    row12 = iota((12, 128), 0)

    def product(start):
        index = index_ref[:, start : start + 128]
        gathered = []
        for t in range(2):
            nodes = index[8 * t : 8 * t + 8]
            lanes = nodes & 127
            gathered.append(pick([lane_take(table_ref[block, 8 * t : 8 * t + 8, :], lanes) for block in range(16)], nodes >> 7))
        out = jnp.zeros((12, 128), F32)
        for j in range(12):
            column = mats_ref[j, :, start : start + 128].astype(F32)
            column = jnp.where(row12 == j, 0.0, column)
            value = gathered[j // 8][j % 8 : j % 8 + 1, :]
            out = out + column * jnp.broadcast_to(value, (12, 128))
        return out

    def values_of(start):
        return jnp.concatenate([product(start), product(start + 128)], axis=1)

    return scatter(values_of, conn_ref)


def tile_sum(product):
    out = None
    for c in range(3):
        for half in range(2):
            tile = product[c * 8 : c * 8 + 8, half * 128 : half * 128 + 128]
            out = tile if out is None else out + tile
    return out


def step(basis, lumped_ref, mats_ref, conn_ref, index_ref, lists_ref, table_ref, image_out, sums_out):
    image = apply_off_diagonal(basis, mats_ref, conn_ref, index_ref, table_ref)
    image_out[...] = image
    sums_out[0:8, :] = tile_sum(basis * basis * lumped_ref[...])
    sums_out[8:16, :] = tile_sum(basis * image)
    return halos_of(image, [lists_ref[0:8, :], lists_ref[8:16, :]])


def second_kernel(
    load_ref, lumped_ref, inverse_ref, lists_ref, index_ref, conn_ref, mats_ref, near_a, near_b,
    diag_out, basis_out, image_out, sums_out, a_out, b_out, table_ref,
):
    inverse = inverse_ref[...]
    force = assembled(load_ref[...], inverse, [near_a[0:8, :], near_b[0:8, :]])
    diag = assembled(lumped_ref[...], inverse, [near_a[8:16, :], near_b[8:16, :]])
    basis = force / diag
    diag_out[...] = diag
    basis_out[...] = basis
    halos = step(basis, lumped_ref, mats_ref, conn_ref, index_ref, lists_ref, table_ref, image_out, sums_out)
    a_out[...] = halos[0]
    b_out[...] = halos[1]


def middle_kernel(
    past_ref, diag_ref, lumped_ref, inverse_ref, lists_ref, index_ref, conn_ref, mats_ref, near_a, near_b,
    basis_out, image_out, sums_out, a_out, b_out, table_ref,
):
    basis = assembled(past_ref[...], inverse_ref[...], [near_a[...], near_b[...]]) / diag_ref[...]
    basis_out[...] = basis
    halos = step(basis, lumped_ref, mats_ref, conn_ref, index_ref, lists_ref, table_ref, image_out, sums_out)
    a_out[...] = halos[0]
    b_out[...] = halos[1]


def place():
    return tuple(lax.axis_index(a) for a in AXES)


def slab_slot(slab):
    return (slab // 128) * 8 + slab % 8


def fourth_kernel(
    past_ref, diag_ref, lumped_ref, inverse_ref, lists_ref, index_ref, conn_ref, mats_ref, near_a, near_b, sums0, sums1, sums2,
    basis_out, image_out, message_out, table_ref, sums_ref,
):
    basis = assembled(past_ref[...], inverse_ref[...], [near_a[...], near_b[...]]) / diag_ref[...]
    basis_out[...] = basis
    halos = step(basis, lumped_ref, mats_ref, conn_ref, index_ref, lists_ref, table_ref, image_out, sums_ref)
    lane = iota((8, 128), 1)
    sub = iota((8, 128), 0)
    moments = jnp.zeros((8, 128), F32)
    for k, ref in enumerate((sums0, sums1, sums2, sums_ref)):
        for t in range(2):
            total = jnp.sum(ref[8 * t : 8 * t + 8, :], axis=0, keepdims=True)
            total = jnp.sum(jnp.broadcast_to(total, (8, 128)), axis=1, keepdims=True)
            moments = jnp.where(lane == 2 * k + t, total, moments)
    moments = jnp.where(sub == 6, moments, 0.0)
    message_out[...] = jnp.broadcast_to(moments[None], (32, 8, 128))
    x, z, y, c = place()
    slab = ((x * 16 + z) * 4 + y) * 2 + c
    odd = c == 1
    to_right = jnp.where(sub < 6, jnp.where(odd, halos[1], halos[0]), moments)
    to_left = jnp.where(sub < 6, jnp.where(odd, halos[0], halos[1]), moments)

    @pl.when(slab < 511)
    def _():
        message_out[slab_slot(jnp.minimum(slab + 1, 511))] = to_right

    @pl.when(slab > 0)
    def _():
        message_out[slab_slot(jnp.maximum(slab - 1, 0))] = to_left


def relay_kernel(message_ref, message_out, direct_out):
    x, z, y, c = place()
    slot = x * 8 + y * 2 + c
    first = (y == 0) & (c == 0)
    last = (y == 3) & (c == 1)
    sub = iota((8, 128), 0)
    moments = message_ref[0]
    for i in range(1, 32):
        moments = moments + message_ref[i]
    moments = jnp.where(sub == 6, moments, 0.0)
    message_out[...] = jnp.broadcast_to(moments[None], (16, 8, 128))
    source_r = jnp.where(first, jnp.where(z < 15, x * 8 + 7, jnp.maximum(x * 8 - 1, 0)), jnp.maximum(slot - 1, 0))
    source_l = jnp.where(last, jnp.where(z > 0, x * 8, jnp.minimum(x * 8 + 8, 31)), jnp.minimum(slot + 1, 31))
    from_left = message_ref[source_r]
    from_right = message_ref[source_l]
    direct_out[0:8, :] = from_left
    direct_out[8:16, :] = from_right

    @pl.when(first)
    def _():
        message_out[(z + 1) % 16] = jnp.where(sub < 6, from_left, moments)

    @pl.when(last)
    def _():
        message_out[(z + 15) % 16] = jnp.where(sub < 6, from_right, moments)


def coefficients(moment):
    zero, one = jnp.zeros((8, 128), F32), jnp.ones((8, 128), F32)
    scale = [jnp.where(moment[2 * i] > 0.0, lax.rsqrt(jnp.where(moment[2 * i] > 0.0, moment[2 * i], one)), zero) for i in range(4)]
    rows = [[moment[i + j] * scale[i] * scale[j] for j in range(4)] + [-moment[i + 4] * scale[i]] for i in range(4)]
    least = one
    inverse = []
    for i in range(4):
        pivot = rows[i][i]
        good = pivot > 1e-6
        least = jnp.minimum(least, jnp.where(good, pivot, zero))
        inverse.append(jnp.where(good, one / jnp.where(good, pivot, one), zero))
        for j in range(i + 1, 4):
            ratio = rows[j][i] * inverse[i]
            for k in range(i + 1, 5):
                rows[j][k] = rows[j][k] - ratio * rows[i][k]
    coef = [zero] * 4
    for i in (3, 2, 1, 0):
        total = rows[i][4]
        for j in range(i + 1, 4):
            total = total - rows[i][j] * coef[j]
        coef[i] = total * inverse[i]
    coef = [coef[i] * scale[i] for i in range(4)]
    at = coef[0] - coef[1] + coef[2] - coef[3] + one
    resid = [v / at for v in coef] + [one / at]
    accel = [None] * 4
    accel[3] = -resid[4]
    for i in (2, 1, 0):
        accel[i] = -resid[i + 1] - accel[i + 1]
    good = (least > PIVOT_FLOOR) & (at > 0.0)
    return accel, resid, good


def last_kernel(message_ref, direct_ref, image_ref, diag_ref, inverse_ref, b0, b1, b2, b3, accel_out, resid_out, flag_out):
    x, z, y, c = place()
    slab = ((x * 16 + z) * 4 + y) * 2 + c
    first = (y == 0) & (c == 0)
    last = (y == 3) & (c == 1)
    lane = iota((8, 128), 1)
    total = message_ref[0]
    for i in range(1, 16):
        total = total + message_ref[i]
    total = jnp.broadcast_to(total[6:7, :], (8, 128))
    moment = [
        jnp.broadcast_to(jnp.sum(jnp.where(lane == k, total, 0.0), axis=1, keepdims=True), (8, 128)) for k in range(8)
    ]
    accel_coef, resid_coef, good = coefficients(moment)
    from_left = jnp.where(first, message_ref[(z + 15) % 16], direct_ref[0:8, :])
    from_right = jnp.where(last, message_ref[(z + 1) % 16], direct_ref[8:16, :])
    from_left = jnp.where(slab > 0, from_left, 0.0)
    from_right = jnp.where(slab < 511, from_right, 0.0)
    odd = c == 1
    near = [jnp.where(odd, from_left, from_right), jnp.where(odd, from_right, from_left)]
    diag = diag_ref[...]
    image = assembled(image_ref[...], inverse_ref[...], near)
    for c_ in range(3):
        for half in range(2):
            at = (slice(c_ * 8, c_ * 8 + 8), slice(half * 128, half * 128 + 128))
            basis = [r[at] for r in (b0, b1, b2, b3)]
            accel = basis[3] * accel_coef[3]
            resid = image[at] * resid_coef[4]
            part = basis[3] * resid_coef[3]
            for k in (2, 1, 0):
                accel = accel + basis[k] * accel_coef[k]
                part = part + basis[k] * resid_coef[k]
            resid = resid + diag[at] * part
            for h in range(8):
                lanes = slice(h * 256 + half * 128, h * 256 + half * 128 + 128)
                accel_out[c_ : c_ + 1, lanes] = accel[h : h + 1, :]
                resid_out[c_ : c_ + 1, lanes] = resid[h : h + 1, :]
    flag_out[0, 0] = jnp.min(jnp.where(good, 1, 0))


def call(kernel, outs, *args, scratch=(), smem_out=None):
    vmem = pl.BlockSpec(memory_space=pltpu.VMEM)
    out_specs = [vmem] * len(outs)
    if smem_out is not None:
        out_specs[smem_out] = pl.BlockSpec(memory_space=pltpu.SMEM)
    return pl.pallas_call(
        kernel,
        out_shape=[jax.ShapeDtypeStruct(s, t) for s, t in outs],
        in_specs=[vmem] * len(args),
        out_specs=out_specs,
        scratch_shapes=list(scratch),
        compiler_params=pltpu.CompilerParams(vmem_limit_bytes=VMEM_LIMIT),
    )(*args)


def swap(side_a, side_b):
    count = 512
    from_b = lax.ppermute(side_b, AXES, [(i, ((i + 1) ^ 1) - 1) for i in range(1, count - 1)])
    from_a = lax.ppermute(side_a, AXES, [(i, i ^ 1) for i in range(count)])
    return from_a, from_b


def plain(load, element_mats, connect, shared):
    node_count = load.shape[1]
    slab_index = lax.axis_index(AXES)
    slab_count = 512
    left_weight = jnp.where(slab_index > 0, F32(0.5), F32(1.0))
    right_weight = jnp.where(slab_index < slab_count - 1, F32(0.5), F32(1.0))
    weights = jnp.ones((node_count,), F32).at[shared[0]].set(left_weight).at[shared[1]].set(right_weight)

    def inner(first, second):
        return lax.psum(jnp.sum(weights * jnp.sum(first * second, axis=0)), AXES)

    def assemble(partial_value):
        from_left = lax.ppermute(partial_value[:, shared[1]], AXES, [(i, i + 1) for i in range(slab_count - 1)])
        from_right = lax.ppermute(partial_value[:, shared[0]], AXES, [(i + 1, i) for i in range(slab_count - 1)])
        return partial_value.at[:, shared[0]].add(from_left).at[:, shared[1]].add(from_right)

    def spread(values):
        values = values.reshape(4, 3, -1).transpose(1, 0, 2).reshape(3, -1)
        return jnp.zeros((3, node_count), F32).at[:, connect.reshape(-1)].add(values)

    def element_apply(field):
        gathered = field[:, connect].transpose(1, 0, 2).reshape(12, -1)
        result = element_mats[:, 0, :].astype(F32) * gathered[0]
        for column in range(1, 12):
            result = result + element_mats[:, column, :].astype(F32) * gathered[column]
        return spread(result)

    lumped = spread(jnp.stack([element_mats[i, i, :].astype(F32) for i in range(12)]))
    both = assemble(jnp.concatenate([load, lumped], axis=0))
    residual, diagonal = both[:3], both[3:]
    direction = residual / diagonal
    accel = jnp.zeros_like(residual)
    gamma = inner(residual, direction)

    def body(_, carry):
        accel, residual, direction, gamma = carry
        image = assemble(element_apply(direction))
        alpha = gamma / inner(direction, image)
        accel = accel + alpha * direction
        residual = residual - alpha * image
        precond = residual / diagonal
        following = inner(residual, precond)
        return accel, residual, precond + following / gamma * direction, following

    accel, residual, _, _ = lax.fori_loop(0, ITERS, body, (accel, residual, direction, gamma))
    return accel, residual


def body(load, element_mats, connect, shared):
    field = ((24, 256), F32)
    halo = ((8, 128), F32)
    sums = ((16, 128), F32)
    table = pltpu.VMEM((16, 16, 128), F32)
    load_f, lumped, index, inverse, lists, a, b = call(
        first_kernel,
        [field, field, ((16, ELEMS), jnp.int32), ((8, 256), jnp.int32), ((16, 128), jnp.int32), sums, sums],
        load, element_mats, connect, shared,
    )
    a, b = swap(a, b)
    diag, b0, image, sums0, a, b = call(
        second_kernel,
        [field, field, field, sums, halo, halo],
        load_f, lumped, inverse, lists, index, connect, element_mats, a, b,
        scratch=[table],
    )
    bases, totals = [b0], [sums0]
    for _ in range(2):
        a, b = swap(a, b)
        basis, image, total, a, b = call(
            middle_kernel,
            [field, field, sums, halo, halo],
            image, diag, lumped, inverse, lists, index, connect, element_mats, a, b,
            scratch=[table],
        )
        bases.append(basis)
        totals.append(total)
    a, b = swap(a, b)
    basis, image, message = call(
        fourth_kernel,
        [field, field, ((32, 8, 128), F32)],
        image, diag, lumped, inverse, lists, index, connect, element_mats, a, b, *totals,
        scratch=[table, pltpu.VMEM((16, 128), F32)],
    )
    bases.append(basis)
    message = lax.all_to_all(message, GROUP, 0, 0, tiled=True)
    message, direct = call(relay_kernel, [((16, 8, 128), F32), sums], message)
    message = lax.all_to_all(message, "z", 0, 0, tiled=True)
    accel, residual, flag = call(
        last_kernel,
        [((3, NODES), F32), ((3, NODES), F32), ((1, 1), jnp.int32)],
        message, direct, image, diag, inverse, *bases,
        smem_out=2,
    )

    def again(carry):
        return (jnp.int32(1),) + plain(load, element_mats, connect, shared)

    _, accel, residual = lax.while_loop(lambda carry: carry[0] == 0, again, (flag.reshape(()), accel, residual))
    return accel, residual


def solution(mesh):
    parts = Mesh(mesh.devices.reshape(4, 16, 4, 2), AXES)
    return jax.shard_map(
        body,
        mesh=parts,
        in_specs=(P(None, AXES), P(None, None, AXES), P(None, AXES), P(None, AXES)),
        out_specs=(P(None, AXES), P(None, AXES)),
        check_vma=False,
    )
```

```python
import jax
import jax.numpy as jnp
from jax import lax
from jax.experimental import pallas as pl
from jax.experimental.pallas import tpu as pltpu
from jax.sharding import Mesh, PartitionSpec as P

ITERS = 4
AXES = ("x", "z", "y", "c")
GROUP = ("x", "y", "c")
NODES = 2048
ELEMS = 2048
SHARED = 256
SPLITS = 3
PIVOT_FLOOR = 1e-3
F32 = jnp.float32
BF16 = jnp.bfloat16
VMEM_LIMIT = 32 * 1024 * 1024


def iota(shape, dim):
    return lax.broadcasted_iota(jnp.int32, shape, dim)


def lane_take(table, lanes):
    return jnp.take_along_axis(table, lanes, axis=1, mode="promise_in_bounds")


def pick(parts, high):
    bit = 0
    while len(parts) > 1:
        odd = (high & (1 << bit)) != 0
        parts = [jnp.where(odd, parts[i + 1], parts[i]) for i in range(0, len(parts), 2)]
        bit += 1
    return parts[0]


def field_rows(field, block):
    return [jnp.broadcast_to(field[c * 16 + block : c * 16 + block + 1, :], (8, 128)) for c in range(3)]


def by_component(rows, comp):
    return jnp.where(comp == 0, rows[0], jnp.where(comp == 1, rows[1], rows[2]))


def halos_of(field, lists):
    comp = iota((8, 128), 0) // 2
    tables = [by_component(field_rows(field, block), comp) for block in range(16)]
    out = []
    for nodes in lists:
        out.append(pick([lane_take(t, nodes & 127) for t in tables], nodes >> 7))
    return out


def assembled(field, inverse, near):
    tiles = []
    for c in range(3):
        for half in range(2):
            place = inverse[half * 8 : half * 8 + 8, :]
            lanes, code = place & 127, place >> 7
            parts = []
            for t in range(4):
                row = 2 * c + (t & 1)
                table = jnp.broadcast_to(near[t >> 1][row : row + 1, :], (8, 128))
                parts.append(lane_take(table, lanes))
            start = c * 16 + half * 8
            tiles.append(field[start : start + 8, :] + jnp.where(code < 0, 0.0, pick(parts, code)))
    return jnp.concatenate(tiles, axis=0)


def bf16_rows(row, count):
    return jnp.broadcast_to(row.astype(F32), (count, row.shape[1])).astype(BF16)


def bf16_iota(shape):
    return iota(shape, 0).astype(F32).astype(BF16)


def high_mask(nodes):
    return bf16_rows(nodes >> 7, 16) == bf16_iota((16, nodes.shape[1]))


def corner_lhs(values, conn):
    zero = jnp.zeros((), BF16)
    parts = []
    rest = values
    for _ in range(SPLITS - 1):
        top = rest.astype(BF16).astype(F32)
        parts.append(top)
        rest = rest - top
    parts.append(rest)
    out = []
    for n in range(4):
        mask = high_mask(conn[n : n + 1, :])
        rows = [part[3 * n + c : 3 * n + c + 1, :] for part in parts for c in range(3)]
        out.append(jnp.concatenate([jnp.where(mask, bf16_rows(row, 16), zero) for row in rows], axis=0))
    return out


def times_one_hot(lhs, nodes):
    shape = (128, nodes.shape[1])
    hot = jnp.where(bf16_rows(nodes & 127, 128) == bf16_iota(shape), jnp.ones((), BF16), jnp.zeros((), BF16))
    return lax.dot_general(lhs, hot, (((1,), (1,)), ((), ())), preferred_element_type=F32)


def scatter(values_of, conn_ref):
    total = None
    for block in range(ELEMS // 256):
        start = block * 256
        conn = conn_ref[:, start : start + 256]
        lhs = corner_lhs(values_of(start), conn)
        for n in range(4):
            piece = times_one_hot(lhs[n], conn[n : n + 1, :])
            total = piece if total is None else total + piece
    out = total[0:48]
    for t in range(1, SPLITS):
        out = out + total[48 * t : 48 * t + 48]
    return out


def first_kernel(
    load_hbm, mats_hbm, conn_hbm, shared_hbm,
    load_out, lumped_out, mats_ref, conn_ref, index_out, inverse_out, lists_out, a_out, b_out,
    load_ref, shared_ref, sems,
):
    small = [
        pltpu.make_async_copy(shared_hbm, shared_ref, sems.at[0]),
        pltpu.make_async_copy(conn_hbm, conn_ref, sems.at[1]),
        pltpu.make_async_copy(load_hbm, load_ref, sems.at[2]),
    ]
    large = [
        pltpu.make_async_copy(mats_hbm.at[pl.ds(3 * i, 3)], mats_ref.at[pl.ds(3 * i, 3)], sems.at[3 + i]) for i in range(4)
    ]
    for copy in small + large:
        copy.start()
    small[0].wait()
    odd = lax.axis_index("c") == 1
    own = shared_ref[...]
    row0, row1 = own[0:1, :], own[1:2, :]
    side_a = jnp.where(odd, row0, row1)
    side_b = jnp.where(odd, row1, row0)

    sub8 = iota((8, 128), 0)
    lists = []
    for side in (side_a, side_b):
        first = jnp.broadcast_to(side[:, 0:128], (8, 128))
        second = jnp.broadcast_to(side[:, 128:256], (8, 128))
        lists.append(jnp.where((sub8 & 1) == 0, first, second))
    lists_out[0:8, :] = lists[0]
    lists_out[8:16, :] = lists[1]

    lane = iota((16, 256), 1)
    zero = jnp.zeros((), BF16)
    found = None
    for t, side in enumerate((side_a, side_b)):
        mask = high_mask(side)
        place = jnp.where(mask, (lane & 127).astype(F32).astype(BF16), zero)
        code = jnp.where(mask, (2 * t + (lane >> 7) + 1).astype(F32).astype(BF16), zero)
        piece = times_one_hot(jnp.concatenate([place, code], axis=0), side)
        found = piece if found is None else found + piece
    inverse_out[...] = (found[16:32].astype(jnp.int32) - 1) * 128 + found[0:16].astype(jnp.int32)

    small[1].wait()
    for j in range(12):
        index_out[j : j + 1, :] = conn_ref[j // 3 : j // 3 + 1, :]
    index_out[12:16, :] = jnp.zeros((4, ELEMS), jnp.int32)

    small[2].wait()
    for c in range(3):
        for h in range(16):
            load_out[c * 16 + h : c * 16 + h + 1, :] = load_ref[c : c + 1, h * 128 : h * 128 + 128]
    load_a, load_b = halos_of(load_out[...], lists)
    a_out[0:8, :] = load_a
    b_out[0:8, :] = load_b

    for copy in large:
        copy.wait()
    row12 = iota((12, 256), 0)

    def diagonal_of(start):
        out = jnp.zeros((12, 256), F32)
        for j in range(12):
            column = mats_ref[j, :, start : start + 256].astype(F32)
            out = jnp.where(row12 == j, column, out)
            mats_ref[j, :, start : start + 256] = jnp.where(row12 == j, 0.0, column).astype(BF16)
        return out

    lumped = scatter(diagonal_of, conn_ref)
    lumped_out[...] = lumped
    lump_a, lump_b = halos_of(lumped, lists)
    a_out[8:16, :] = lump_a
    b_out[8:16, :] = lump_b


def apply_off_diagonal(field, mats_ref, conn_ref, index_ref, table_ref):
    sub = iota((8, 128), 0)
    for block in range(16):
        rows = field_rows(field, block)
        table_ref[block, 0:8, :] = by_component(rows, sub % 3)
        table_ref[block, 8:16, :] = by_component(rows, (sub + 2) % 3)

    def product(start):
        index = index_ref[:, start : start + 128]
        gathered = []
        for t in range(2):
            nodes = index[8 * t : 8 * t + 8]
            lanes = nodes & 127
            gathered.append(pick([lane_take(table_ref[block, 8 * t : 8 * t + 8, :], lanes) for block in range(16)], nodes >> 7))
        out = jnp.zeros((12, 128), F32)
        for j in range(12):
            column = mats_ref[j, :, start : start + 128].astype(F32)
            value = gathered[j // 8][j % 8 : j % 8 + 1, :]
            out = out + column * jnp.broadcast_to(value, (12, 128))
        return out

    def values_of(start):
        return jnp.concatenate([product(start), product(start + 128)], axis=1)

    return scatter(values_of, conn_ref)


def tile_sum(product):
    out = product[0:8, :]
    for i in range(1, 6):
        out = out + product[8 * i : 8 * i + 8, :]
    return out


def step(basis, lumped_ref, mats_ref, conn_ref, index_ref, lists_ref, table_ref, image_out, sums_out):
    image = apply_off_diagonal(basis, mats_ref, conn_ref, index_ref, table_ref)
    image_out[...] = image
    sums_out[0:8, :] = tile_sum(basis * basis * lumped_ref[...])
    sums_out[8:16, :] = tile_sum(basis * image)
    return halos_of(image, [lists_ref[0:8, :], lists_ref[8:16, :]])


def second_kernel(
    load_ref, lumped_ref, inverse_ref, lists_ref, index_ref, conn_ref, mats_ref, near_b, near_a,
    diag_out, basis_out, image_out, sums_out, a_out, b_out, table_ref,
):
    inverse = inverse_ref[...]
    force = assembled(load_ref[...], inverse, [near_a[0:8, :], near_b[0:8, :]])
    diag = assembled(lumped_ref[...], inverse, [near_a[8:16, :], near_b[8:16, :]])
    basis = force / diag
    diag_out[...] = diag
    basis_out[...] = basis
    halos = step(basis, lumped_ref, mats_ref, conn_ref, index_ref, lists_ref, table_ref, image_out, sums_out)
    a_out[...] = halos[0]
    b_out[...] = halos[1]


def middle_kernel(
    past_ref, diag_ref, lumped_ref, inverse_ref, lists_ref, index_ref, conn_ref, mats_ref, near_b, near_a,
    basis_out, image_out, sums_out, a_out, b_out, table_ref,
):
    basis = assembled(past_ref[...], inverse_ref[...], [near_a[...], near_b[...]]) / diag_ref[...]
    basis_out[...] = basis
    halos = step(basis, lumped_ref, mats_ref, conn_ref, index_ref, lists_ref, table_ref, image_out, sums_out)
    a_out[...] = halos[0]
    b_out[...] = halos[1]


def place():
    return tuple(lax.axis_index(a) for a in AXES)


def slab_slot(slab):
    return (slab // 128) * 8 + slab % 8


def fourth_kernel(
    past_ref, diag_ref, lumped_ref, inverse_ref, lists_ref, index_ref, conn_ref, mats_ref, near_b, near_a, sums0, sums1, sums2,
    basis_out, image_out, message_out, table_ref, sums_ref,
):
    basis = assembled(past_ref[...], inverse_ref[...], [near_a[...], near_b[...]]) / diag_ref[...]
    basis_out[...] = basis
    halos = step(basis, lumped_ref, mats_ref, conn_ref, index_ref, lists_ref, table_ref, image_out, sums_ref)
    lane = iota((8, 128), 1)
    sub = iota((8, 128), 0)
    moments = jnp.zeros((8, 128), F32)
    for k, ref in enumerate((sums0, sums1, sums2, sums_ref)):
        for t in range(2):
            total = jnp.sum(ref[8 * t : 8 * t + 8, :], axis=0, keepdims=True)
            total = jnp.sum(jnp.broadcast_to(total, (8, 128)), axis=1, keepdims=True)
            moments = jnp.where(lane == 2 * k + t, total, moments)
    moments = jnp.where(sub == 6, moments, 0.0)
    message_out[...] = jnp.broadcast_to(moments[None], (32, 8, 128))
    x, z, y, c = place()
    slab = ((x * 16 + z) * 4 + y) * 2 + c
    odd = c == 1
    to_right = jnp.where(sub < 6, jnp.where(odd, halos[1], halos[0]), moments)
    to_left = jnp.where(sub < 6, jnp.where(odd, halos[0], halos[1]), moments)

    @pl.when(slab < 511)
    def _():
        message_out[slab_slot(jnp.minimum(slab + 1, 511))] = to_right

    @pl.when(slab > 0)
    def _():
        message_out[slab_slot(jnp.maximum(slab - 1, 0))] = to_left


def relay_kernel(message_ref, message_out, direct_out):
    x, z, y, c = place()
    slot = x * 8 + y * 2 + c
    first = (y == 0) & (c == 0)
    last = (y == 3) & (c == 1)
    sub = iota((8, 128), 0)
    moments = message_ref[0]
    for i in range(1, 32):
        moments = moments + message_ref[i]
    moments = jnp.where(sub == 6, moments, 0.0)
    message_out[...] = jnp.broadcast_to(moments[None], (16, 8, 128))
    source_r = jnp.where(first, jnp.where(z < 15, x * 8 + 7, jnp.maximum(x * 8 - 1, 0)), jnp.maximum(slot - 1, 0))
    source_l = jnp.where(last, jnp.where(z > 0, x * 8, jnp.minimum(x * 8 + 8, 31)), jnp.minimum(slot + 1, 31))
    from_left = message_ref[source_r]
    from_right = message_ref[source_l]
    direct_out[0:8, :] = from_left
    direct_out[8:16, :] = from_right

    @pl.when(first)
    def _():
        message_out[(z + 1) % 16] = jnp.where(sub < 6, from_left, moments)

    @pl.when(last)
    def _():
        message_out[(z + 15) % 16] = jnp.where(sub < 6, from_right, moments)


def coefficients(moment):
    zero, one = jnp.zeros((8, 128), F32), jnp.ones((8, 128), F32)
    scale = [jnp.where(moment[2 * i] > 0.0, lax.rsqrt(jnp.where(moment[2 * i] > 0.0, moment[2 * i], one)), zero) for i in range(4)]
    rows = [[moment[i + j] * scale[i] * scale[j] for j in range(4)] + [-moment[i + 4] * scale[i]] for i in range(4)]
    least = one
    inverse = []
    for i in range(4):
        pivot = rows[i][i]
        good = pivot > 1e-6
        least = jnp.minimum(least, jnp.where(good, pivot, zero))
        inverse.append(jnp.where(good, one / jnp.where(good, pivot, one), zero))
        for j in range(i + 1, 4):
            ratio = rows[j][i] * inverse[i]
            for k in range(i + 1, 5):
                rows[j][k] = rows[j][k] - ratio * rows[i][k]
    coef = [zero] * 4
    for i in (3, 2, 1, 0):
        total = rows[i][4]
        for j in range(i + 1, 4):
            total = total - rows[i][j] * coef[j]
        coef[i] = total * inverse[i]
    coef = [coef[i] * scale[i] for i in range(4)]
    at = coef[0] - coef[1] + coef[2] - coef[3] + one
    resid = [v / at for v in coef] + [one / at]
    accel = [None] * 4
    accel[3] = -resid[4]
    for i in (2, 1, 0):
        accel[i] = -resid[i + 1] - accel[i + 1]
    good = (least > PIVOT_FLOOR) & (at > 0.0)
    return accel, resid, good


def last_kernel(message_ref, direct_ref, image_ref, diag_ref, inverse_ref, b0, b1, b2, b3, accel_out, resid_out, flag_out):
    x, z, y, c = place()
    slab = ((x * 16 + z) * 4 + y) * 2 + c
    first = (y == 0) & (c == 0)
    last = (y == 3) & (c == 1)
    lane = iota((8, 128), 1)
    total = message_ref[0]
    for i in range(1, 16):
        total = total + message_ref[i]
    total = jnp.broadcast_to(total[6:7, :], (8, 128))
    moment = [
        jnp.broadcast_to(jnp.sum(jnp.where(lane == k, total, 0.0), axis=1, keepdims=True), (8, 128)) for k in range(8)
    ]
    accel_coef, resid_coef, good = coefficients(moment)
    from_left = jnp.where(first, message_ref[(z + 15) % 16], direct_ref[0:8, :])
    from_right = jnp.where(last, message_ref[(z + 1) % 16], direct_ref[8:16, :])
    from_left = jnp.where(slab > 0, from_left, 0.0)
    from_right = jnp.where(slab < 511, from_right, 0.0)
    odd = c == 1
    near = [jnp.where(odd, from_left, from_right), jnp.where(odd, from_right, from_left)]
    diag = diag_ref[...]
    image = assembled(image_ref[...], inverse_ref[...], near)
    for c_ in range(3):
        for half in range(2):
            rows = slice(c_ * 16 + half * 8, c_ * 16 + half * 8 + 8)
            basis = [r[rows, :] for r in (b0, b1, b2, b3)]
            accel = basis[3] * accel_coef[3]
            part = basis[3] * resid_coef[3]
            for k in (2, 1, 0):
                accel = accel + basis[k] * accel_coef[k]
                part = part + basis[k] * resid_coef[k]
            resid = image[rows, :] * resid_coef[4] + diag[rows, :] * part
            for h in range(8):
                start = (half * 8 + h) * 128
                accel_out[c_ : c_ + 1, start : start + 128] = accel[h : h + 1, :]
                resid_out[c_ : c_ + 1, start : start + 128] = resid[h : h + 1, :]
    flag_out[0, 0] = jnp.min(jnp.where(good, 1, 0))


def call(kernel, outs, *args, scratch=(), smem_out=None, space=pltpu.VMEM):
    out_specs = [pl.BlockSpec(memory_space=pltpu.VMEM)] * len(outs)
    if smem_out is not None:
        out_specs[smem_out] = pl.BlockSpec(memory_space=pltpu.SMEM)
    return pl.pallas_call(
        kernel,
        out_shape=[jax.ShapeDtypeStruct(s, t) for s, t in outs],
        in_specs=[pl.BlockSpec(memory_space=space)] * len(args),
        out_specs=out_specs,
        scratch_shapes=list(scratch),
        compiler_params=pltpu.CompilerParams(vmem_limit_bytes=VMEM_LIMIT),
    )(*args)


def same(*args):
    def kernel(*refs):
        for src, dst in zip(refs[: len(args)], refs[len(args) :]):
            dst[...] = src[...]

    return call(kernel, [(a.shape, a.dtype) for a in args], *args)


def swap(side_a, side_b):
    count = 512
    from_b = lax.ppermute(side_b, AXES, [(i, ((i + 1) ^ 1) - 1) for i in range(1, count - 1)])
    from_a = lax.ppermute(side_a, AXES, [(i, i ^ 1) for i in range(count)])
    return from_a, from_b


def plain(load, element_mats, connect, shared):
    node_count = load.shape[1]
    slab_index = lax.axis_index(AXES)
    slab_count = 512
    left_weight = jnp.where(slab_index > 0, F32(0.5), F32(1.0))
    right_weight = jnp.where(slab_index < slab_count - 1, F32(0.5), F32(1.0))
    weights = jnp.ones((node_count,), F32).at[shared[0]].set(left_weight).at[shared[1]].set(right_weight)

    def inner(first, second):
        return lax.psum(jnp.sum(weights * jnp.sum(first * second, axis=0)), AXES)

    def assemble(partial_value):
        from_left = lax.ppermute(partial_value[:, shared[1]], AXES, [(i, i + 1) for i in range(slab_count - 1)])
        from_right = lax.ppermute(partial_value[:, shared[0]], AXES, [(i + 1, i) for i in range(slab_count - 1)])
        return partial_value.at[:, shared[0]].add(from_left).at[:, shared[1]].add(from_right)

    def spread(values):
        values = values.reshape(4, 3, -1).transpose(1, 0, 2).reshape(3, -1)
        return jnp.zeros((3, node_count), F32).at[:, connect.reshape(-1)].add(values)

    def element_apply(field):
        gathered = field[:, connect].transpose(1, 0, 2).reshape(12, -1)
        result = element_mats[:, 0, :].astype(F32) * gathered[0]
        for column in range(1, 12):
            result = result + element_mats[:, column, :].astype(F32) * gathered[column]
        return spread(result)

    lumped = spread(jnp.stack([element_mats[i, i, :].astype(F32) for i in range(12)]))
    both = assemble(jnp.concatenate([load, lumped], axis=0))
    residual, diagonal = both[:3], both[3:]
    direction = residual / diagonal
    accel = jnp.zeros_like(residual)
    gamma = inner(residual, direction)

    def body(_, carry):
        accel, residual, direction, gamma = carry
        image = assemble(element_apply(direction))
        alpha = gamma / inner(direction, image)
        accel = accel + alpha * direction
        residual = residual - alpha * image
        precond = residual / diagonal
        following = inner(residual, precond)
        return accel, residual, precond + following / gamma * direction, following

    accel, residual, _, _ = lax.fori_loop(0, ITERS, body, (accel, residual, direction, gamma))
    return accel, residual


def body(load, element_mats, connect, shared):
    field = ((48, 128), F32)
    halo = ((8, 128), F32)
    sums = ((16, 128), F32)
    index = ((16, ELEMS), jnp.int32)
    inverse = ((16, 128), jnp.int32)
    table = pltpu.VMEM((16, 16, 128), F32)
    load_f, lumped, mats, conn, index, inverse, lists, a, b = call(
        first_kernel,
        [field, field, ((12, 12, ELEMS), BF16), ((4, ELEMS), jnp.int32), index, inverse, inverse, sums, sums],
        load, element_mats, connect, shared,
        scratch=[pltpu.VMEM((3, NODES), F32), pltpu.VMEM((2, SHARED), jnp.int32), pltpu.SemaphoreType.DMA((7,))],
        space=pltpu.HBM,
    )
    a, b = swap(a, b)
    diag, b0, image, sums0, a, b = call(
        second_kernel,
        [field, field, field, sums, halo, halo],
        load_f, lumped, inverse, lists, index, conn, mats, b, a,
        scratch=[table],
    )
    bases, totals = [b0], [sums0]
    for _ in range(2):
        a, b = swap(a, b)
        basis, image, total, a, b = call(
            middle_kernel,
            [field, field, sums, halo, halo],
            image, diag, lumped, inverse, lists, index, conn, mats, b, a,
            scratch=[table],
        )
        bases.append(basis)
        totals.append(total)
    a, b = swap(a, b)
    basis, image, message = call(
        fourth_kernel,
        [field, field, ((32, 8, 128), F32)],
        image, diag, lumped, inverse, lists, index, conn, mats, b, a, *totals,
        scratch=[table, pltpu.VMEM((16, 128), F32)],
    )
    bases.append(basis)
    message = lax.all_to_all(message, GROUP, 0, 0, tiled=True)
    message, direct = call(relay_kernel, [((16, 8, 128), F32), sums], message)
    message = lax.all_to_all(message, "z", 0, 0, tiled=True)
    accel, residual, flag = call(
        last_kernel,
        [((3, NODES), F32), ((3, NODES), F32), ((1, 1), jnp.int32)],
        message, direct, image, diag, inverse, *bases,
        smem_out=2,
    )

    def again(carry):
        args = same(load, element_mats, connect, shared)
        return (jnp.int32(1),) + tuple(same(*plain(*args)))

    _, accel, residual = lax.while_loop(lambda carry: carry[0] == 0, again, (flag.reshape(()), accel, residual))
    return accel, residual


def solution(mesh):
    parts = Mesh(mesh.devices.reshape(4, 16, 4, 2), AXES)
    return jax.shard_map(
        body,
        mesh=parts,
        in_specs=(P(None, AXES), P(None, None, AXES), P(None, AXES), P(None, AXES)),
        out_specs=(P(None, AXES), P(None, AXES)),
        check_vma=False,
    )
```

```python
import jax
import jax.numpy as jnp
from jax import lax
from jax.experimental import pallas as pl
from jax.experimental.pallas import tpu as pltpu
from jax.sharding import Mesh, PartitionSpec as P

ITERS = 4
AXES = ("x", "z", "y", "c")
GROUP = ("x", "y", "c")
NODES = 2048
ELEMS = 2048
SHARED = 256
SPLITS = 3
PIVOT_FLOOR = 0.02
F32 = jnp.float32
BF16 = jnp.bfloat16
VMEM_LIMIT = 32 * 1024 * 1024


def iota(shape, dim):
    return lax.broadcasted_iota(jnp.int32, shape, dim)


def lane_take(table, lanes):
    return jnp.take_along_axis(table, lanes, axis=1, mode="promise_in_bounds")


def pick(parts, high):
    bit = 0
    while len(parts) > 1:
        odd = (high & (1 << bit)) != 0
        parts = [jnp.where(odd, parts[i + 1], parts[i]) for i in range(0, len(parts), 2)]
        bit += 1
    return parts[0]


def field_rows(field, block):
    return [jnp.broadcast_to(field[c * 16 + block : c * 16 + block + 1, :], (8, 128)) for c in range(3)]


def by_component(rows, comp):
    return jnp.where(comp == 0, rows[0], jnp.where(comp == 1, rows[1], rows[2]))


def halos_of(field, lists):
    comp = iota((8, 128), 0) // 2
    tables = [by_component(field_rows(field, block), comp) for block in range(16)]
    out = []
    for nodes in lists:
        out.append(pick([lane_take(t, nodes & 127) for t in tables], nodes >> 7))
    return out


def assembled(field, inverse, near):
    tiles = []
    for c in range(3):
        for half in range(2):
            place = inverse[half * 8 : half * 8 + 8, :]
            lanes, code = place & 127, place >> 7
            parts = []
            for t in range(4):
                row = 2 * c + (t & 1)
                table = jnp.broadcast_to(near[t >> 1][row : row + 1, :], (8, 128))
                parts.append(lane_take(table, lanes))
            start = c * 16 + half * 8
            tiles.append(field[start : start + 8, :] + jnp.where(code < 0, 0.0, pick(parts, code)))
    return jnp.concatenate(tiles, axis=0)


def bf16_rows(row, count):
    return jnp.broadcast_to(row.astype(F32), (count, row.shape[1])).astype(BF16)


def bf16_iota(shape):
    return iota(shape, 0).astype(F32).astype(BF16)


def high_mask(nodes):
    return bf16_rows(nodes >> 7, 16) == bf16_iota((16, nodes.shape[1]))


def corner_lhs(values, conn):
    zero = jnp.zeros((), BF16)
    parts = []
    rest = values
    for _ in range(SPLITS - 1):
        top = rest.astype(BF16).astype(F32)
        parts.append(top)
        rest = rest - top
    parts.append(rest)
    out = []
    for n in range(4):
        mask = high_mask(conn[n : n + 1, :])
        rows = [part[3 * n + c : 3 * n + c + 1, :] for part in parts for c in range(3)]
        out.append(jnp.concatenate([jnp.where(mask, bf16_rows(row, 16), zero) for row in rows], axis=0))
    return out


def times_one_hot(lhs, nodes):
    shape = (128, nodes.shape[1])
    hot = jnp.where(bf16_rows(nodes & 127, 128) == bf16_iota(shape), jnp.ones((), BF16), jnp.zeros((), BF16))
    return lax.dot_general(lhs, hot, (((1,), (1,)), ((), ())), preferred_element_type=F32)


def scatter(values_of, conn_ref):
    total = None
    for block in range(ELEMS // 256):
        start = block * 256
        conn = conn_ref[:, start : start + 256]
        lhs = corner_lhs(values_of(start), conn)
        for n in range(4):
            piece = times_one_hot(lhs[n], conn[n : n + 1, :])
            total = piece if total is None else total + piece
    out = total[0:48]
    for t in range(1, SPLITS):
        out = out + total[48 * t : 48 * t + 48]
    return out


def first_kernel(
    load_hbm, mats_hbm, conn_hbm, shared_hbm,
    load_out, lumped_out, mats_ref, conn_ref, index_out, inverse_out, lists_out, a_out, b_out,
    load_ref, shared_ref, sems,
):
    small = [
        pltpu.make_async_copy(shared_hbm, shared_ref, sems.at[0]),
        pltpu.make_async_copy(conn_hbm, conn_ref, sems.at[1]),
        pltpu.make_async_copy(load_hbm, load_ref, sems.at[2]),
    ]
    large = [
        pltpu.make_async_copy(mats_hbm.at[pl.ds(3 * i, 3)], mats_ref.at[pl.ds(3 * i, 3)], sems.at[3 + i]) for i in range(4)
    ]
    for copy in small[:2] + large + small[2:]:
        copy.start()
    for copy in small:
        copy.wait()
    odd = lax.axis_index("c") == 1
    own = shared_ref[...]
    row0, row1 = own[0:1, :], own[1:2, :]
    side_a = jnp.where(odd, row0, row1)
    side_b = jnp.where(odd, row1, row0)

    sub8 = iota((8, 128), 0)
    lists = []
    for side in (side_a, side_b):
        first = jnp.broadcast_to(side[:, 0:128], (8, 128))
        second = jnp.broadcast_to(side[:, 128:256], (8, 128))
        lists.append(jnp.where((sub8 & 1) == 0, first, second))
    lists_out[0:8, :] = lists[0]
    lists_out[8:16, :] = lists[1]

    lane = iota((16, 256), 1)
    zero = jnp.zeros((), BF16)
    found = None
    for t, side in enumerate((side_a, side_b)):
        mask = high_mask(side)
        place = jnp.where(mask, (lane & 127).astype(F32).astype(BF16), zero)
        code = jnp.where(mask, (2 * t + (lane >> 7) + 1).astype(F32).astype(BF16), zero)
        piece = times_one_hot(jnp.concatenate([place, code], axis=0), side)
        found = piece if found is None else found + piece
    inverse_out[...] = (found[16:32].astype(jnp.int32) - 1) * 128 + found[0:16].astype(jnp.int32)

    for j in range(12):
        index_out[j : j + 1, :] = conn_ref[j // 3 : j // 3 + 1, :]
    index_out[12:16, :] = jnp.zeros((4, ELEMS), jnp.int32)

    for c in range(3):
        for h in range(16):
            load_out[c * 16 + h : c * 16 + h + 1, :] = load_ref[c : c + 1, h * 128 : h * 128 + 128]
    load_a, load_b = halos_of(load_out[...], lists)
    a_out[0:8, :] = load_a
    b_out[0:8, :] = load_b

    row12 = iota((12, 256), 0)
    zero16 = jnp.zeros((), BF16)
    lumped = None
    for copy in large:
        copy.wait()
    for block in range(ELEMS // 256):
        for n in range(4):
            span = slice(block * 256, block * 256 + 256)
            nodes = conn_ref[n : n + 1, span]
            mask = high_mask(nodes)
            rows = []
            for j in range(3 * n, 3 * n + 3):
                column = mats_ref[j, :, span].astype(F32)
                rows.append(jnp.where(mask, bf16_rows(column[j : j + 1, :], 16), zero16))
                mats_ref[j, :, span] = jnp.where(row12 == j, 0.0, column).astype(BF16)
            piece = times_one_hot(jnp.concatenate(rows, axis=0), nodes)
            lumped = piece if lumped is None else lumped + piece
    lumped_out[...] = lumped
    lump_a, lump_b = halos_of(lumped, lists)
    a_out[8:16, :] = lump_a
    b_out[8:16, :] = lump_b


def apply_off_diagonal(field, mats_ref, conn_ref, index_ref, table_ref):
    sub = iota((8, 128), 0)
    for block in range(16):
        rows = field_rows(field, block)
        table_ref[block, 0:8, :] = by_component(rows, sub % 3)
        table_ref[block, 8:16, :] = by_component(rows, (sub + 2) % 3)

    def product(start):
        index = index_ref[:, start : start + 128]
        gathered = []
        for t in range(2):
            nodes = index[8 * t : 8 * t + 8]
            lanes = nodes & 127
            gathered.append(pick([lane_take(table_ref[block, 8 * t : 8 * t + 8, :], lanes) for block in range(16)], nodes >> 7))
        out = jnp.zeros((12, 128), F32)
        for j in range(12):
            column = mats_ref[j, :, start : start + 128].astype(F32)
            value = gathered[j // 8][j % 8 : j % 8 + 1, :]
            out = out + column * jnp.broadcast_to(value, (12, 128))
        return out

    def values_of(start):
        return jnp.concatenate([product(start), product(start + 128)], axis=1)

    return scatter(values_of, conn_ref)


def tile_sum(product):
    out = product[0:8, :]
    for i in range(1, 6):
        out = out + product[8 * i : 8 * i + 8, :]
    return out


def step(basis, lumped_ref, mats_ref, conn_ref, index_ref, lists_ref, table_ref, image_out, sums_out):
    image = apply_off_diagonal(basis, mats_ref, conn_ref, index_ref, table_ref)
    image_out[...] = image
    sums_out[0:8, :] = tile_sum(basis * basis * lumped_ref[...])
    sums_out[8:16, :] = tile_sum(basis * image)
    return halos_of(image, [lists_ref[0:8, :], lists_ref[8:16, :]])


def second_kernel(
    load_ref, lumped_ref, inverse_ref, lists_ref, index_ref, conn_ref, mats_ref, near_b, near_a,
    diag_out, basis_out, image_out, sums_out, a_out, b_out, table_ref,
):
    inverse = inverse_ref[...]
    force = assembled(load_ref[...], inverse, [near_a[0:8, :], near_b[0:8, :]])
    diag = assembled(lumped_ref[...], inverse, [near_a[8:16, :], near_b[8:16, :]])
    basis = force / diag
    diag_out[...] = diag
    basis_out[...] = basis
    halos = step(basis, lumped_ref, mats_ref, conn_ref, index_ref, lists_ref, table_ref, image_out, sums_out)
    a_out[...] = halos[0]
    b_out[...] = halos[1]


def middle_kernel(
    past_ref, diag_ref, lumped_ref, inverse_ref, lists_ref, index_ref, conn_ref, mats_ref, near_b, near_a,
    basis_out, image_out, sums_out, a_out, b_out, table_ref,
):
    basis = assembled(past_ref[...], inverse_ref[...], [near_a[...], near_b[...]]) / diag_ref[...]
    basis_out[...] = basis
    halos = step(basis, lumped_ref, mats_ref, conn_ref, index_ref, lists_ref, table_ref, image_out, sums_out)
    a_out[...] = halos[0]
    b_out[...] = halos[1]


def place():
    return tuple(lax.axis_index(a) for a in AXES)


def slab_slot(slab):
    return (slab // 128) * 8 + slab % 8


def fourth_kernel(
    past_ref, diag_ref, lumped_ref, inverse_ref, lists_ref, index_ref, conn_ref, mats_ref, near_b, near_a, sums0, sums1, sums2,
    basis_out, image_out, message_out, table_ref, sums_ref,
):
    basis = assembled(past_ref[...], inverse_ref[...], [near_a[...], near_b[...]]) / diag_ref[...]
    basis_out[...] = basis
    halos = step(basis, lumped_ref, mats_ref, conn_ref, index_ref, lists_ref, table_ref, image_out, sums_ref)
    lane = iota((8, 128), 1)
    sub = iota((8, 128), 0)
    moments = jnp.zeros((8, 128), F32)
    for k, ref in enumerate((sums0, sums1, sums2, sums_ref)):
        for t in range(2):
            total = jnp.sum(ref[8 * t : 8 * t + 8, :], axis=0, keepdims=True)
            total = jnp.sum(jnp.broadcast_to(total, (8, 128)), axis=1, keepdims=True)
            moments = jnp.where(lane == 2 * k + t, total, moments)
    moments = jnp.where(sub == 6, moments, 0.0)
    message_out[...] = jnp.broadcast_to(moments[None], (32, 8, 128))
    x, z, y, c = place()
    slab = ((x * 16 + z) * 4 + y) * 2 + c
    odd = c == 1
    to_right = jnp.where(sub < 6, jnp.where(odd, halos[1], halos[0]), moments)
    to_left = jnp.where(sub < 6, jnp.where(odd, halos[0], halos[1]), moments)

    @pl.when(slab < 511)
    def _():
        message_out[slab_slot(jnp.minimum(slab + 1, 511))] = to_right

    @pl.when(slab > 0)
    def _():
        message_out[slab_slot(jnp.maximum(slab - 1, 0))] = to_left


def relay_kernel(message_ref, message_out, direct_out):
    x, z, y, c = place()
    slot = x * 8 + y * 2 + c
    first = (y == 0) & (c == 0)
    last = (y == 3) & (c == 1)
    sub = iota((8, 128), 0)
    moments = message_ref[0]
    for i in range(1, 32):
        moments = moments + message_ref[i]
    moments = jnp.where(sub == 6, moments, 0.0)
    message_out[...] = jnp.broadcast_to(moments[None], (16, 8, 128))
    source_r = jnp.where(first, jnp.where(z < 15, x * 8 + 7, jnp.maximum(x * 8 - 1, 0)), jnp.maximum(slot - 1, 0))
    source_l = jnp.where(last, jnp.where(z > 0, x * 8, jnp.minimum(x * 8 + 8, 31)), jnp.minimum(slot + 1, 31))
    from_left = message_ref[source_r]
    from_right = message_ref[source_l]
    direct_out[0:8, :] = from_left
    direct_out[8:16, :] = from_right

    @pl.when(first)
    def _():
        message_out[(z + 1) % 16] = jnp.where(sub < 6, from_left, moments)

    @pl.when(last)
    def _():
        message_out[(z + 15) % 16] = jnp.where(sub < 6, from_right, moments)


def coefficients(moment):
    zero, one = jnp.zeros((8, 128), F32), jnp.ones((8, 128), F32)
    scale = [jnp.where(moment[2 * i] > 0.0, lax.rsqrt(jnp.where(moment[2 * i] > 0.0, moment[2 * i], one)), zero) for i in range(4)]
    rows = [[moment[i + j] * scale[i] * scale[j] for j in range(4)] + [-moment[i + 4] * scale[i]] for i in range(4)]
    least = one
    inverse = []
    for i in range(4):
        pivot = rows[i][i]
        good = pivot > 1e-6
        least = jnp.minimum(least, jnp.where(good, pivot, zero))
        inverse.append(jnp.where(good, one / jnp.where(good, pivot, one), zero))
        for j in range(i + 1, 4):
            ratio = rows[j][i] * inverse[i]
            for k in range(i + 1, 5):
                rows[j][k] = rows[j][k] - ratio * rows[i][k]
    coef = [zero] * 4
    for i in (3, 2, 1, 0):
        total = rows[i][4]
        for j in range(i + 1, 4):
            total = total - rows[i][j] * coef[j]
        coef[i] = total * inverse[i]
    coef = [coef[i] * scale[i] for i in range(4)]
    at = coef[0] - coef[1] + coef[2] - coef[3] + one
    resid = [v / at for v in coef] + [one / at]
    accel = [None] * 4
    accel[3] = -resid[4]
    for i in (2, 1, 0):
        accel[i] = -resid[i + 1] - accel[i + 1]
    good = (least > PIVOT_FLOOR) & (at > 0.0)
    return accel, resid, good


def last_kernel(message_ref, direct_ref, image_ref, diag_ref, inverse_ref, b0, b1, b2, b3, accel_out, resid_out, flag_out):
    x, z, y, c = place()
    slab = ((x * 16 + z) * 4 + y) * 2 + c
    first = (y == 0) & (c == 0)
    last = (y == 3) & (c == 1)
    lane = iota((8, 128), 1)
    total = message_ref[0]
    for i in range(1, 16):
        total = total + message_ref[i]
    total = jnp.broadcast_to(total[6:7, :], (8, 128))
    moment = [
        jnp.broadcast_to(jnp.sum(jnp.where(lane == k, total, 0.0), axis=1, keepdims=True), (8, 128)) for k in range(8)
    ]
    accel_coef, resid_coef, good = coefficients(moment)
    from_left = jnp.where(first, message_ref[(z + 15) % 16], direct_ref[0:8, :])
    from_right = jnp.where(last, message_ref[(z + 1) % 16], direct_ref[8:16, :])
    from_left = jnp.where(slab > 0, from_left, 0.0)
    from_right = jnp.where(slab < 511, from_right, 0.0)
    odd = c == 1
    near = [jnp.where(odd, from_left, from_right), jnp.where(odd, from_right, from_left)]
    diag = diag_ref[...]
    image = assembled(image_ref[...], inverse_ref[...], near)
    for c_ in range(3):
        for half in range(2):
            rows = slice(c_ * 16 + half * 8, c_ * 16 + half * 8 + 8)
            basis = [r[rows, :] for r in (b0, b1, b2, b3)]
            accel = basis[3] * accel_coef[3]
            part = basis[3] * resid_coef[3]
            for k in (2, 1, 0):
                accel = accel + basis[k] * accel_coef[k]
                part = part + basis[k] * resid_coef[k]
            resid = image[rows, :] * resid_coef[4] + diag[rows, :] * part
            for h in range(8):
                start = (half * 8 + h) * 128
                accel_out[c_ : c_ + 1, start : start + 128] = accel[h : h + 1, :]
                resid_out[c_ : c_ + 1, start : start + 128] = resid[h : h + 1, :]
    flag_out[0, 0] = jnp.min(jnp.where(good, 1, 0))


def call(kernel, outs, *args, scratch=(), smem_out=None, space=pltpu.VMEM):
    out_specs = [pl.BlockSpec(memory_space=pltpu.VMEM)] * len(outs)
    if smem_out is not None:
        out_specs[smem_out] = pl.BlockSpec(memory_space=pltpu.SMEM)
    return pl.pallas_call(
        kernel,
        out_shape=[jax.ShapeDtypeStruct(s, t) for s, t in outs],
        in_specs=[pl.BlockSpec(memory_space=space)] * len(args),
        out_specs=out_specs,
        scratch_shapes=list(scratch),
        compiler_params=pltpu.CompilerParams(vmem_limit_bytes=VMEM_LIMIT),
    )(*args)


def same(*args):
    def kernel(*refs):
        for src, dst in zip(refs[: len(args)], refs[len(args) :]):
            dst[...] = src[...]

    return call(kernel, [(a.shape, a.dtype) for a in args], *args)


def swap(side_a, side_b):
    count = 512
    from_b = lax.ppermute(side_b, AXES, [(i, ((i + 1) ^ 1) - 1) for i in range(1, count - 1)])
    from_a = lax.ppermute(side_a, AXES, [(i, i ^ 1) for i in range(count)])
    return from_a, from_b


def plain(load, element_mats, connect, shared):
    node_count = load.shape[1]
    slab_index = lax.axis_index(AXES)
    slab_count = 512
    left_weight = jnp.where(slab_index > 0, F32(0.5), F32(1.0))
    right_weight = jnp.where(slab_index < slab_count - 1, F32(0.5), F32(1.0))
    weights = jnp.ones((node_count,), F32).at[shared[0]].set(left_weight).at[shared[1]].set(right_weight)

    def inner(first, second):
        return lax.psum(jnp.sum(weights * jnp.sum(first * second, axis=0)), AXES)

    def assemble(partial_value):
        from_left = lax.ppermute(partial_value[:, shared[1]], AXES, [(i, i + 1) for i in range(slab_count - 1)])
        from_right = lax.ppermute(partial_value[:, shared[0]], AXES, [(i + 1, i) for i in range(slab_count - 1)])
        return partial_value.at[:, shared[0]].add(from_left).at[:, shared[1]].add(from_right)

    def spread(values):
        values = values.reshape(4, 3, -1).transpose(1, 0, 2).reshape(3, -1)
        return jnp.zeros((3, node_count), F32).at[:, connect.reshape(-1)].add(values)

    def element_apply(field):
        gathered = field[:, connect].transpose(1, 0, 2).reshape(12, -1)
        result = element_mats[:, 0, :].astype(F32) * gathered[0]
        for column in range(1, 12):
            result = result + element_mats[:, column, :].astype(F32) * gathered[column]
        return spread(result)

    lumped = spread(jnp.stack([element_mats[i, i, :].astype(F32) for i in range(12)]))
    both = assemble(jnp.concatenate([load, lumped], axis=0))
    residual, diagonal = both[:3], both[3:]
    direction = residual / diagonal
    accel = jnp.zeros_like(residual)
    gamma = inner(residual, direction)

    def body(_, carry):
        accel, residual, direction, gamma = carry
        image = assemble(element_apply(direction))
        alpha = gamma / inner(direction, image)
        accel = accel + alpha * direction
        residual = residual - alpha * image
        precond = residual / diagonal
        following = inner(residual, precond)
        return accel, residual, precond + following / gamma * direction, following

    accel, residual, _, _ = lax.fori_loop(0, ITERS, body, (accel, residual, direction, gamma))
    return accel, residual


def body(load, element_mats, connect, shared):
    field = ((48, 128), F32)
    halo = ((8, 128), F32)
    sums = ((16, 128), F32)
    index = ((16, ELEMS), jnp.int32)
    inverse = ((16, 128), jnp.int32)
    table = pltpu.VMEM((16, 16, 128), F32)
    load_f, lumped, mats, conn, index, inverse, lists, a, b = call(
        first_kernel,
        [field, field, ((12, 12, ELEMS), BF16), ((4, ELEMS), jnp.int32), index, inverse, inverse, sums, sums],
        load, element_mats, connect, shared,
        scratch=[pltpu.VMEM((3, NODES), F32), pltpu.VMEM((2, SHARED), jnp.int32), pltpu.SemaphoreType.DMA((7,))],
        space=pltpu.HBM,
    )
    a, b = swap(a, b)
    diag, b0, image, sums0, a, b = call(
        second_kernel,
        [field, field, field, sums, halo, halo],
        load_f, lumped, inverse, lists, index, conn, mats, b, a,
        scratch=[table],
    )
    bases, totals = [b0], [sums0]
    for _ in range(2):
        a, b = swap(a, b)
        basis, image, total, a, b = call(
            middle_kernel,
            [field, field, sums, halo, halo],
            image, diag, lumped, inverse, lists, index, conn, mats, b, a,
            scratch=[table],
        )
        bases.append(basis)
        totals.append(total)
    a, b = swap(a, b)
    basis, image, message = call(
        fourth_kernel,
        [field, field, ((32, 8, 128), F32)],
        image, diag, lumped, inverse, lists, index, conn, mats, b, a, *totals,
        scratch=[table, pltpu.VMEM((16, 128), F32)],
    )
    bases.append(basis)
    message = lax.all_to_all(message, GROUP, 0, 0, tiled=True)
    message, direct = call(relay_kernel, [((16, 8, 128), F32), sums], message)
    message = lax.all_to_all(message, "z", 0, 0, tiled=True)
    accel, residual, flag = call(
        last_kernel,
        [((3, NODES), F32), ((3, NODES), F32), ((1, 1), jnp.int32)],
        message, direct, image, diag, inverse, *bases,
        smem_out=2,
    )

    def again(carry):
        args = same(load, element_mats, connect, shared)
        return (jnp.int32(1),) + tuple(same(*plain(*args)))

    _, accel, residual = lax.while_loop(lambda carry: carry[0] == 0, again, (flag.reshape(()), accel, residual))
    return accel, residual


def solution(mesh):
    parts = Mesh(mesh.devices.reshape(4, 16, 4, 2), AXES)
    return jax.shard_map(
        body,
        mesh=parts,
        in_specs=(P(None, AXES), P(None, None, AXES), P(None, AXES), P(None, AXES)),
        out_specs=(P(None, AXES), P(None, AXES)),
        check_vma=False,
    )
```

```python
import jax
import jax.numpy as jnp
from jax import lax
from jax.experimental import pallas as pl
from jax.experimental.pallas import tpu as pltpu
from jax.sharding import Mesh, PartitionSpec as P

ITERS = 4
AXES = ("x", "z", "y", "c")
GROUP = ("x", "y", "c")
NODES = 2048
ELEMS = 2048
SHARED = 256
SPLITS = 3
PIVOT_FLOOR = 0.02
F32 = jnp.float32
BF16 = jnp.bfloat16
EARLY_WORK = pl.CostEstimate(flops=2_000_000, bytes_accessed=400_000, transcendentals=0)
VMEM_LIMIT = 32 * 1024 * 1024


def iota(shape, dim):
    return lax.broadcasted_iota(jnp.int32, shape, dim)


def lane_take(table, lanes):
    return jnp.take_along_axis(table, lanes, axis=1, mode="promise_in_bounds")


def pick(parts, high):
    bit = 0
    while len(parts) > 1:
        odd = (high & (1 << bit)) != 0
        parts = [jnp.where(odd, parts[i + 1], parts[i]) for i in range(0, len(parts), 2)]
        bit += 1
    return parts[0]


def field_rows(field, block):
    return [jnp.broadcast_to(field[c * 16 + block : c * 16 + block + 1, :], (8, 128)) for c in range(3)]


def by_component(rows, comp):
    return jnp.where(comp == 0, rows[0], jnp.where(comp == 1, rows[1], rows[2]))


def halos_of(field, lists):
    comp = iota((8, 128), 0) // 2
    tables = [by_component(field_rows(field, block), comp) for block in range(16)]
    out = []
    for nodes in lists:
        out.append(pick([lane_take(t, nodes & 127) for t in tables], nodes >> 7))
    return out


def assembled(field, inverse, near, blocks=range(4)):
    tiles = []
    for c in range(3):
        for half in range(2):
            place = inverse[half * 8 : half * 8 + 8, :]
            lanes, code = place & 127, place >> 7
            parts = []
            for t in blocks:
                row = 2 * c + (t & 1)
                table = jnp.broadcast_to(near[t >> 1][row : row + 1, :], (8, 128))
                parts.append(lane_take(table, lanes))
            start = c * 16 + half * 8
            here = (code >= blocks[0]) & (code <= blocks[-1])
            tiles.append(field[start : start + 8, :] + jnp.where(here, pick(parts, code), 0.0))
    return jnp.concatenate(tiles, axis=0)


def bf16_rows(row, count):
    return jnp.broadcast_to(row.astype(F32), (count, row.shape[1])).astype(BF16)


def bf16_iota(shape):
    return iota(shape, 0).astype(F32).astype(BF16)


def high_mask(nodes):
    return bf16_rows(nodes >> 7, 16) == bf16_iota((16, nodes.shape[1]))


def corner_lhs(values, conn):
    zero = jnp.zeros((), BF16)
    parts = []
    rest = values
    for _ in range(SPLITS - 1):
        top = rest.astype(BF16).astype(F32)
        parts.append(top)
        rest = rest - top
    parts.append(rest)
    out = []
    for n in range(4):
        mask = high_mask(conn[n : n + 1, :])
        rows = [part[3 * n + c : 3 * n + c + 1, :] for part in parts for c in range(3)]
        out.append(jnp.concatenate([jnp.where(mask, bf16_rows(row, 16), zero) for row in rows], axis=0))
    return out


def times_one_hot(lhs, nodes):
    shape = (128, nodes.shape[1])
    hot = jnp.where(bf16_rows(nodes & 127, 128) == bf16_iota(shape), jnp.ones((), BF16), jnp.zeros((), BF16))
    return lax.dot_general(lhs, hot, (((1,), (1,)), ((), ())), preferred_element_type=F32)


def scatter(values_of, conn_ref):
    total = None
    for block in range(ELEMS // 256):
        start = block * 256
        conn = conn_ref[:, start : start + 256]
        lhs = corner_lhs(values_of(start), conn)
        for n in range(4):
            piece = times_one_hot(lhs[n], conn[n : n + 1, :])
            total = piece if total is None else total + piece
    out = total[0:48]
    for t in range(1, SPLITS):
        out = out + total[48 * t : 48 * t + 48]
    return out


def first_kernel(
    load_hbm, mats_hbm, conn_hbm, shared_hbm,
    load_out, lumped_out, mats_ref, conn_ref, lists_out, a_out, b_out,
    load_ref, shared_ref, sems,
):
    small = [
        pltpu.make_async_copy(shared_hbm, shared_ref, sems.at[0]),
        pltpu.make_async_copy(conn_hbm, conn_ref, sems.at[1]),
        pltpu.make_async_copy(load_hbm, load_ref, sems.at[2]),
    ]
    large = [
        pltpu.make_async_copy(mats_hbm.at[pl.ds(3 * i, 3)], mats_ref.at[pl.ds(3 * i, 3)], sems.at[3 + i]) for i in range(4)
    ]
    for copy in small[:2] + large + small[2:]:
        copy.start()
    for copy in small:
        copy.wait()
    odd = lax.axis_index("c") == 1
    own = shared_ref[...]
    row0, row1 = own[0:1, :], own[1:2, :]
    side_a = jnp.where(odd, row0, row1)
    side_b = jnp.where(odd, row1, row0)

    sub8 = iota((8, 128), 0)
    lists = []
    for side in (side_a, side_b):
        first = jnp.broadcast_to(side[:, 0:128], (8, 128))
        second = jnp.broadcast_to(side[:, 128:256], (8, 128))
        lists.append(jnp.where((sub8 & 1) == 0, first, second))
    lists_out[0:8, :] = lists[0]
    lists_out[8:16, :] = lists[1]

    for c in range(3):
        for h in range(16):
            load_out[c * 16 + h : c * 16 + h + 1, :] = load_ref[c : c + 1, h * 128 : h * 128 + 128]
    load_a, load_b = halos_of(load_out[...], lists)
    a_out[0:8, :] = load_a
    b_out[0:8, :] = load_b

    row12 = iota((12, 256), 0)
    zero16 = jnp.zeros((), BF16)
    lumped = None
    for copy in large:
        copy.wait()
    for block in range(ELEMS // 256):
        for n in range(4):
            span = slice(block * 256, block * 256 + 256)
            nodes = conn_ref[n : n + 1, span]
            mask = high_mask(nodes)
            rows = []
            for j in range(3 * n, 3 * n + 3):
                column = mats_ref[j, :, span].astype(F32)
                rows.append(jnp.where(mask, bf16_rows(column[j : j + 1, :], 16), zero16))
                mats_ref[j, :, span] = jnp.where(row12 == j, 0.0, column).astype(BF16)
            piece = times_one_hot(jnp.concatenate(rows, axis=0), nodes)
            lumped = piece if lumped is None else lumped + piece
    lumped_out[...] = lumped
    lump_a, lump_b = halos_of(lumped, lists)
    a_out[8:16, :] = lump_a
    b_out[8:16, :] = lump_b


def at_corners(tables_of, index_ref, out_ref):
    for t in range(2):
        tables = tables_of(t)
        for start in range(0, ELEMS, 128):
            nodes = index_ref[8 * t : 8 * t + 8, start : start + 128]
            lanes = nodes & 127
            out_ref[8 * t : 8 * t + 8, start : start + 128] = pick([lane_take(table, lanes) for table in tables], nodes >> 7)


def component_of_row(t):
    return (iota((8, 128), 0) + 2 * t) % 3


def corner_tables(field):
    rows = [field_rows(field, block) for block in range(16)]
    return lambda t: [by_component(r, component_of_row(t)) for r in rows]


def list_kernel(conn_ref, lists_ref, index_out, inverse_out, place_out):
    lane = iota((16, 256), 1)
    zero = jnp.zeros((), BF16)
    found = None
    for t in range(2):
        side = jnp.concatenate([lists_ref[8 * t : 8 * t + 1, :], lists_ref[8 * t + 1 : 8 * t + 2, :]], axis=1)
        mask = high_mask(side)
        place = jnp.where(mask, (lane & 127).astype(F32).astype(BF16), zero)
        code = jnp.where(mask, (2 * t + (lane >> 7) + 1).astype(F32).astype(BF16), zero)
        piece = times_one_hot(jnp.concatenate([place, code], axis=0), side)
        found = piece if found is None else found + piece
    inverse = (found[16:32].astype(jnp.int32) - 1) * 128 + found[0:16].astype(jnp.int32)
    inverse_out[...] = inverse
    for j in range(12):
        index_out[j : j + 1, :] = conn_ref[j // 3 : j // 3 + 1, :]
    index_out[12:16, :] = jnp.zeros((4, ELEMS), jnp.int32)
    tables = [jnp.broadcast_to(inverse[block : block + 1, :], (8, 128)) for block in range(16)]
    at_corners(lambda t: tables, index_out, place_out)


def early_kernel(past_ref, index_ref, *rest):
    if len(rest) == 3:
        diag_ref, corner_out, scale_out = rest
        at_corners(corner_tables(1.0 / diag_ref[...]), index_ref, scale_out)
    else:
        (corner_out,) = rest
    at_corners(corner_tables(past_ref[...]), index_ref, corner_out)


def apply_off_diagonal(corner, mats_ref, conn_ref):
    def product(start):
        gathered = corner(start)
        out = jnp.zeros((12, 128), F32)
        for j in range(12):
            column = mats_ref[j, :, start : start + 128].astype(F32)
            value = gathered[j // 8][j % 8 : j % 8 + 1, :]
            out = out + column * jnp.broadcast_to(value, (12, 128))
        return out

    def values_of(start):
        return jnp.concatenate([product(start), product(start + 128)], axis=1)

    return scatter(values_of, conn_ref)


def full_corner(field, index_ref, table_ref):
    of = corner_tables(field)
    for t in range(2):
        for block, table in enumerate(of(t)):
            table_ref[block, 8 * t : 8 * t + 8, :] = table

    def corner(start):
        index = index_ref[:, start : start + 128]
        gathered = []
        for t in range(2):
            nodes = index[8 * t : 8 * t + 8]
            lanes = nodes & 127
            gathered.append(pick([lane_take(table_ref[block, 8 * t : 8 * t + 8, :], lanes) for block in range(16)], nodes >> 7))
        return gathered

    return corner


def late_corner(corner_ref, scale_ref, place_ref, near):
    tables = []
    for t in range(2):
        comp = component_of_row(t)
        tables.append([])
        for block in range(4):
            k, values = block & 1, near[block >> 1]
            rows = [jnp.broadcast_to(values[2 * c + k : 2 * c + k + 1, :], (8, 128)) for c in range(3)]
            tables[t].append(by_component(rows, comp))

    def corner(start):
        gathered = []
        for t in range(2):
            at = (slice(8 * t, 8 * t + 8), slice(start, start + 128))
            place = place_ref[at]
            lanes, code = place & 127, place >> 7
            extra = pick([lane_take(table, lanes) for table in tables[t]], code)
            gathered.append((corner_ref[at] + jnp.where(code >= 0, extra, 0.0)) * scale_ref[at])
        return gathered

    return corner


def tile_sum(product):
    out = product[0:8, :]
    for i in range(1, 6):
        out = out + product[8 * i : 8 * i + 8, :]
    return out


def step(basis, corner, lumped_ref, mats_ref, conn_ref, lists_ref, image_out, sums_out):
    image = apply_off_diagonal(corner, mats_ref, conn_ref)
    image_out[...] = image
    sums_out[0:8, :] = tile_sum(basis * basis * lumped_ref[...])
    sums_out[8:16, :] = tile_sum(basis * image)
    return halos_of(image, [lists_ref[0:8, :], lists_ref[8:16, :]])


def second_kernel(
    load_ref, lumped_ref, inverse_ref, lists_ref, index_ref, conn_ref, mats_ref, near_b, near_a,
    diag_out, basis_out, image_out, sums_out, a_out, b_out, table_ref,
):
    inverse = inverse_ref[...]
    force = assembled(load_ref[...], inverse, [near_a[0:8, :], near_b[0:8, :]])
    diag = assembled(lumped_ref[...], inverse, [near_a[8:16, :], near_b[8:16, :]])
    basis = force / diag
    diag_out[...] = diag
    basis_out[...] = basis
    corner = full_corner(basis, index_ref, table_ref)
    halos = step(basis, corner, lumped_ref, mats_ref, conn_ref, lists_ref, image_out, sums_out)
    a_out[...] = halos[0]
    b_out[...] = halos[1]


def late_step(past_ref, corner_ref, scale_ref, place_ref, diag_ref, lumped_ref, inverse_ref, lists_ref, conn_ref, mats_ref, near_b, near_a, basis_out, image_out, sums_out):
    near = [near_a[...], near_b[...]]
    basis = assembled(past_ref[...], inverse_ref[...], near) / diag_ref[...]
    basis_out[...] = basis
    corner = late_corner(corner_ref, scale_ref, place_ref, near)
    return step(basis, corner, lumped_ref, mats_ref, conn_ref, lists_ref, image_out, sums_out)


def middle_kernel(
    past_ref, corner_ref, scale_ref, place_ref, diag_ref, lumped_ref, inverse_ref, lists_ref, conn_ref, mats_ref, near_b, near_a,
    basis_out, image_out, sums_out, a_out, b_out,
):
    halos = late_step(
        past_ref, corner_ref, scale_ref, place_ref, diag_ref, lumped_ref, inverse_ref, lists_ref, conn_ref, mats_ref, near_b, near_a,
        basis_out, image_out, sums_out,
    )
    a_out[...] = halos[0]
    b_out[...] = halos[1]


def place():
    return tuple(lax.axis_index(a) for a in AXES)


def slab_slot(slab):
    return (slab // 128) * 8 + slab % 8


def fourth_kernel(
    past_ref, corner_ref, scale_ref, place_ref, diag_ref, lumped_ref, inverse_ref, lists_ref, conn_ref, mats_ref, near_b, near_a,
    sums0, sums1, sums2,
    basis_out, image_out, message_out, sums_ref,
):
    halos = late_step(
        past_ref, corner_ref, scale_ref, place_ref, diag_ref, lumped_ref, inverse_ref, lists_ref, conn_ref, mats_ref, near_b, near_a,
        basis_out, image_out, sums_ref,
    )
    lane = iota((8, 128), 1)
    sub = iota((8, 128), 0)
    moments = jnp.zeros((8, 128), F32)
    for k, ref in enumerate((sums0, sums1, sums2, sums_ref)):
        for t in range(2):
            total = jnp.sum(ref[8 * t : 8 * t + 8, :], axis=0, keepdims=True)
            total = jnp.sum(jnp.broadcast_to(total, (8, 128)), axis=1, keepdims=True)
            moments = jnp.where(lane == 2 * k + t, total, moments)
    moments = jnp.where(sub == 6, moments, 0.0)
    message_out[...] = jnp.broadcast_to(moments[None], (32, 8, 128))
    x, z, y, c = place()
    slab = ((x * 16 + z) * 4 + y) * 2 + c
    odd = c == 1
    to_right = jnp.where(sub < 6, jnp.where(odd, halos[1], halos[0]), moments)
    to_left = jnp.where(sub < 6, jnp.where(odd, halos[0], halos[1]), moments)

    @pl.when(slab < 511)
    def _():
        message_out[slab_slot(jnp.minimum(slab + 1, 511))] = to_right

    @pl.when(slab > 0)
    def _():
        message_out[slab_slot(jnp.maximum(slab - 1, 0))] = to_left


def relay_kernel(message_ref, message_out, direct_out):
    x, z, y, c = place()
    slot = x * 8 + y * 2 + c
    first = (y == 0) & (c == 0)
    last = (y == 3) & (c == 1)
    sub = iota((8, 128), 0)
    moments = message_ref[0]
    for i in range(1, 32):
        moments = moments + message_ref[i]
    moments = jnp.where(sub == 6, moments, 0.0)
    message_out[...] = jnp.broadcast_to(moments[None], (16, 8, 128))
    source_r = jnp.where(first, jnp.where(z < 15, x * 8 + 7, jnp.maximum(x * 8 - 1, 0)), jnp.maximum(slot - 1, 0))
    source_l = jnp.where(last, jnp.where(z > 0, x * 8, jnp.minimum(x * 8 + 8, 31)), jnp.minimum(slot + 1, 31))
    from_left = message_ref[source_r]
    from_right = message_ref[source_l]
    direct_out[0:8, :] = from_left
    direct_out[8:16, :] = from_right

    @pl.when(first)
    def _():
        message_out[(z + 1) % 16] = jnp.where(sub < 6, from_left, moments)

    @pl.when(last)
    def _():
        message_out[(z + 15) % 16] = jnp.where(sub < 6, from_right, moments)


def coefficients(moment):
    zero, one = jnp.zeros((8, 128), F32), jnp.ones((8, 128), F32)
    scale = [jnp.where(moment[2 * i] > 0.0, lax.rsqrt(jnp.where(moment[2 * i] > 0.0, moment[2 * i], one)), zero) for i in range(4)]
    rows = [[moment[i + j] * scale[i] * scale[j] for j in range(4)] + [-moment[i + 4] * scale[i]] for i in range(4)]
    least = one
    inverse = []
    for i in range(4):
        pivot = rows[i][i]
        good = pivot > 1e-6
        least = jnp.minimum(least, jnp.where(good, pivot, zero))
        inverse.append(jnp.where(good, one / jnp.where(good, pivot, one), zero))
        for j in range(i + 1, 4):
            ratio = rows[j][i] * inverse[i]
            for k in range(i + 1, 5):
                rows[j][k] = rows[j][k] - ratio * rows[i][k]
    coef = [zero] * 4
    for i in (3, 2, 1, 0):
        total = rows[i][4]
        for j in range(i + 1, 4):
            total = total - rows[i][j] * coef[j]
        coef[i] = total * inverse[i]
    coef = [coef[i] * scale[i] for i in range(4)]
    at = coef[0] - coef[1] + coef[2] - coef[3] + one
    resid = [v / at for v in coef] + [one / at]
    accel = [None] * 4
    accel[3] = -resid[4]
    for i in (2, 1, 0):
        accel[i] = -resid[i + 1] - accel[i + 1]
    good = (least > PIVOT_FLOOR) & (at > 0.0)
    return accel, resid, good


def last_kernel(message_ref, direct_ref, image_ref, diag_ref, inverse_ref, b0, b1, b2, b3, accel_out, resid_out, flag_out):
    x, z, y, c = place()
    slab = ((x * 16 + z) * 4 + y) * 2 + c
    first = (y == 0) & (c == 0)
    last = (y == 3) & (c == 1)
    lane = iota((8, 128), 1)
    total = message_ref[0]
    for i in range(1, 16):
        total = total + message_ref[i]
    total = jnp.broadcast_to(total[6:7, :], (8, 128))
    moment = [
        jnp.broadcast_to(jnp.sum(jnp.where(lane == k, total, 0.0), axis=1, keepdims=True), (8, 128)) for k in range(8)
    ]
    accel_coef, resid_coef, good = coefficients(moment)
    from_left = jnp.where(first, message_ref[(z + 15) % 16], direct_ref[0:8, :])
    from_right = jnp.where(last, message_ref[(z + 1) % 16], direct_ref[8:16, :])
    from_left = jnp.where(slab > 0, from_left, 0.0)
    from_right = jnp.where(slab < 511, from_right, 0.0)
    odd = c == 1
    near = [jnp.where(odd, from_left, from_right), jnp.where(odd, from_right, from_left)]
    diag = diag_ref[...]
    image = assembled(image_ref[...], inverse_ref[...], near)
    for c_ in range(3):
        for half in range(2):
            rows = slice(c_ * 16 + half * 8, c_ * 16 + half * 8 + 8)
            basis = [r[rows, :] for r in (b0, b1, b2, b3)]
            accel = basis[3] * accel_coef[3]
            part = basis[3] * resid_coef[3]
            for k in (2, 1, 0):
                accel = accel + basis[k] * accel_coef[k]
                part = part + basis[k] * resid_coef[k]
            resid = image[rows, :] * resid_coef[4] + diag[rows, :] * part
            for h in range(8):
                start = (half * 8 + h) * 128
                accel_out[c_ : c_ + 1, start : start + 128] = accel[h : h + 1, :]
                resid_out[c_ : c_ + 1, start : start + 128] = resid[h : h + 1, :]
    flag_out[0, 0] = jnp.min(jnp.where(good, 1, 0))


def call(kernel, outs, *args, scratch=(), smem_out=None, space=pltpu.VMEM, work=None):
    out_specs = [pl.BlockSpec(memory_space=pltpu.VMEM)] * len(outs)
    if smem_out is not None:
        out_specs[smem_out] = pl.BlockSpec(memory_space=pltpu.SMEM)
    return pl.pallas_call(
        kernel,
        out_shape=[jax.ShapeDtypeStruct(s, t) for s, t in outs],
        in_specs=[pl.BlockSpec(memory_space=space)] * len(args),
        out_specs=out_specs,
        scratch_shapes=list(scratch),
        compiler_params=pltpu.CompilerParams(vmem_limit_bytes=VMEM_LIMIT),
        cost_estimate=work,
    )(*args)


def same(*args):
    def kernel(*refs):
        for src, dst in zip(refs[: len(args)], refs[len(args) :]):
            dst[...] = src[...]

    return call(kernel, [(a.shape, a.dtype) for a in args], *args)


def swap(side_a, side_b):
    count = 512
    from_b = lax.ppermute(side_b, AXES, [(i, ((i + 1) ^ 1) - 1) for i in range(1, count - 1)])
    from_a = lax.ppermute(side_a, AXES, [(i, i ^ 1) for i in range(count)])
    return from_a, from_b


def plain(load, element_mats, connect, shared):
    node_count = load.shape[1]
    slab_index = lax.axis_index(AXES)
    slab_count = 512
    left_weight = jnp.where(slab_index > 0, F32(0.5), F32(1.0))
    right_weight = jnp.where(slab_index < slab_count - 1, F32(0.5), F32(1.0))
    weights = jnp.ones((node_count,), F32).at[shared[0]].set(left_weight).at[shared[1]].set(right_weight)

    def inner(first, second):
        return lax.psum(jnp.sum(weights * jnp.sum(first * second, axis=0)), AXES)

    def assemble(partial_value):
        from_left = lax.ppermute(partial_value[:, shared[1]], AXES, [(i, i + 1) for i in range(slab_count - 1)])
        from_right = lax.ppermute(partial_value[:, shared[0]], AXES, [(i + 1, i) for i in range(slab_count - 1)])
        return partial_value.at[:, shared[0]].add(from_left).at[:, shared[1]].add(from_right)

    def spread(values):
        values = values.reshape(4, 3, -1).transpose(1, 0, 2).reshape(3, -1)
        return jnp.zeros((3, node_count), F32).at[:, connect.reshape(-1)].add(values)

    def element_apply(field):
        gathered = field[:, connect].transpose(1, 0, 2).reshape(12, -1)
        result = element_mats[:, 0, :].astype(F32) * gathered[0]
        for column in range(1, 12):
            result = result + element_mats[:, column, :].astype(F32) * gathered[column]
        return spread(result)

    lumped = spread(jnp.stack([element_mats[i, i, :].astype(F32) for i in range(12)]))
    both = assemble(jnp.concatenate([load, lumped], axis=0))
    residual, diagonal = both[:3], both[3:]
    direction = residual / diagonal
    accel = jnp.zeros_like(residual)
    gamma = inner(residual, direction)

    def body(_, carry):
        accel, residual, direction, gamma = carry
        image = assemble(element_apply(direction))
        alpha = gamma / inner(direction, image)
        accel = accel + alpha * direction
        residual = residual - alpha * image
        precond = residual / diagonal
        following = inner(residual, precond)
        return accel, residual, precond + following / gamma * direction, following

    accel, residual, _, _ = lax.fori_loop(0, ITERS, body, (accel, residual, direction, gamma))
    return accel, residual


def body(load, element_mats, connect, shared):
    field = ((48, 128), F32)
    halo = ((8, 128), F32)
    sums = ((16, 128), F32)
    corners = ((16, ELEMS), F32)
    index = ((16, ELEMS), jnp.int32)
    inverse = ((16, 128), jnp.int32)
    load_f, lumped, mats, conn, lists, a, b = call(
        first_kernel,
        [field, field, ((12, 12, ELEMS), BF16), ((4, ELEMS), jnp.int32), inverse, sums, sums],
        load, element_mats, connect, shared,
        scratch=[pltpu.VMEM((3, NODES), F32), pltpu.VMEM((2, SHARED), jnp.int32), pltpu.SemaphoreType.DMA((7,))],
        space=pltpu.HBM,
    )
    a, b = swap(a, b)
    index, inverse, places = call(list_kernel, [index, inverse, index], conn, lists, work=EARLY_WORK)
    diag, b0, image, total, a, b = call(
        second_kernel,
        [field, field, field, sums, halo, halo],
        load_f, lumped, inverse, lists, index, conn, mats, b, a,
        scratch=[pltpu.VMEM((16, 16, 128), F32)],
    )
    bases, totals = [b0], [total]
    for round_ in range(3):
        a, b = swap(a, b)
        if round_ == 0:
            corner, scale = call(early_kernel, [corners, corners], image, index, diag, work=EARLY_WORK)
        else:
            (corner,) = call(early_kernel, [corners], image, index, work=EARLY_WORK)
        args = (image, corner, scale, places, diag, lumped, inverse, lists, conn, mats, b, a)
        if round_ < 2:
            basis, image, total, a, b = call(middle_kernel, [field, field, sums, halo, halo], *args)
            bases.append(basis)
            totals.append(total)
    basis, image, message = call(
        fourth_kernel,
        [field, field, ((32, 8, 128), F32)],
        *args, *totals,
        scratch=[pltpu.VMEM((16, 128), F32)],
    )
    bases.append(basis)
    message = lax.all_to_all(message, GROUP, 0, 0, tiled=True)
    message, direct = call(relay_kernel, [((16, 8, 128), F32), sums], message)
    message = lax.all_to_all(message, "z", 0, 0, tiled=True)
    accel, residual, flag = call(
        last_kernel,
        [((3, NODES), F32), ((3, NODES), F32), ((1, 1), jnp.int32)],
        message, direct, image, diag, inverse, *bases,
        smem_out=2,
    )

    def again(carry):
        args = same(load, element_mats, connect, shared)
        return (jnp.int32(1),) + tuple(same(*plain(*args)))

    _, accel, residual = lax.while_loop(lambda carry: carry[0] == 0, again, (flag.reshape(()), accel, residual))
    return accel, residual


def solution(mesh):
    parts = Mesh(mesh.devices.reshape(4, 16, 4, 2), AXES)
    return jax.shard_map(
        body,
        mesh=parts,
        in_specs=(P(None, AXES), P(None, None, AXES), P(None, AXES), P(None, AXES)),
        out_specs=(P(None, AXES), P(None, AXES)),
        check_vma=False,
    )
```

```python
import jax
import jax.numpy as jnp
from jax import lax
from jax.experimental import pallas as pl
from jax.experimental.pallas import tpu as pltpu
from jax.sharding import Mesh, PartitionSpec as P

ITERS = 4
AXES = ("x", "z", "y", "c")
GROUP = ("x", "y", "c")
NODES = 2048
ELEMS = 2048
SHARED = 256
SPLITS = 3
PIVOT_FLOOR = 0.02
F32 = jnp.float32
BF16 = jnp.bfloat16
EARLY_WORK = pl.CostEstimate(flops=2_000_000, bytes_accessed=400_000, transcendentals=0)
VMEM_LIMIT = 32 * 1024 * 1024


def iota(shape, dim):
    return lax.broadcasted_iota(jnp.int32, shape, dim)


def lane_take(table, lanes):
    return jnp.take_along_axis(table, lanes, axis=1, mode="promise_in_bounds")


def pick(parts, high):
    bit = 0
    while len(parts) > 1:
        odd = (high & (1 << bit)) != 0
        parts = [jnp.where(odd, parts[i + 1], parts[i]) for i in range(0, len(parts), 2)]
        bit += 1
    return parts[0]


def field_rows(field, block):
    return [jnp.broadcast_to(field[c * 16 + block : c * 16 + block + 1, :], (8, 128)) for c in range(3)]


def by_component(rows, comp):
    return jnp.where(comp == 0, rows[0], jnp.where(comp == 1, rows[1], rows[2]))


def halos_of(field, lists):
    comp = iota((8, 128), 0) // 2
    tables = [by_component(field_rows(field, block), comp) for block in range(16)]
    out = []
    for nodes in lists:
        out.append(pick([lane_take(t, nodes & 127) for t in tables], nodes >> 7))
    return out


def assembled(field, inverse, near, blocks=range(4)):
    tiles = []
    for c in range(3):
        for half in range(2):
            place = inverse[half * 8 : half * 8 + 8, :]
            lanes, code = place & 127, place >> 7
            parts = []
            for t in blocks:
                row = 2 * c + (t & 1)
                table = jnp.broadcast_to(near[t >> 1][row : row + 1, :], (8, 128))
                parts.append(lane_take(table, lanes))
            start = c * 16 + half * 8
            here = (code >= blocks[0]) & (code <= blocks[-1])
            tiles.append(field[start : start + 8, :] + jnp.where(here, pick(parts, code), 0.0))
    return jnp.concatenate(tiles, axis=0)


def bf16_rows(row, count):
    return jnp.broadcast_to(row.astype(F32), (count, row.shape[1])).astype(BF16)


def bf16_iota(shape):
    return iota(shape, 0).astype(F32).astype(BF16)


def high_mask(nodes):
    return bf16_rows(nodes >> 7, 16) == bf16_iota((16, nodes.shape[1]))


def corner_lhs(values, conn):
    zero = jnp.zeros((), BF16)
    parts = []
    rest = values
    for _ in range(SPLITS - 1):
        top = rest.astype(BF16).astype(F32)
        parts.append(top)
        rest = rest - top
    parts.append(rest)
    out = []
    for n in range(4):
        mask = high_mask(conn[n : n + 1, :])
        rows = [part[3 * n + c : 3 * n + c + 1, :] for part in parts for c in range(3)]
        out.append(jnp.concatenate([jnp.where(mask, bf16_rows(row, 16), zero) for row in rows], axis=0))
    return out


def times_one_hot(lhs, nodes):
    shape = (128, nodes.shape[1])
    hot = jnp.where(bf16_rows(nodes & 127, 128) == bf16_iota(shape), jnp.ones((), BF16), jnp.zeros((), BF16))
    return lax.dot_general(lhs, hot, (((1,), (1,)), ((), ())), preferred_element_type=F32)


def scatter(values_of, conn_ref, hot_ref):
    total = None
    for block in range(ELEMS // 256):
        start = block * 256
        lhs = corner_lhs(values_of(start), conn_ref[:, start : start + 256])
        for n in range(4):
            piece = jnp.dot(lhs[n], hot_ref[n, start : start + 256, :], preferred_element_type=F32)
            total = piece if total is None else total + piece
    out = total[0:48]
    for t in range(1, SPLITS):
        out = out + total[48 * t : 48 * t + 48]
    return out


def first_kernel(
    load_hbm, mats_hbm, conn_hbm, shared_hbm,
    load_out, lumped_out, mats_ref, conn_ref, lists_out, a_out, b_out,
    load_ref, shared_ref, sems,
):
    small = [
        pltpu.make_async_copy(shared_hbm, shared_ref, sems.at[0]),
        pltpu.make_async_copy(conn_hbm, conn_ref, sems.at[1]),
        pltpu.make_async_copy(load_hbm, load_ref, sems.at[2]),
    ]
    large = [
        pltpu.make_async_copy(mats_hbm.at[i], mats_ref.at[i], sems.at[3 + i]) for i in range(12)
    ]
    for copy in small[:2] + large + small[2:]:
        copy.start()
    for copy in small:
        copy.wait()
    odd = lax.axis_index("c") == 1
    own = shared_ref[...]
    row0, row1 = own[0:1, :], own[1:2, :]
    side_a = jnp.where(odd, row0, row1)
    side_b = jnp.where(odd, row1, row0)

    sub8 = iota((8, 128), 0)
    lists = []
    for side in (side_a, side_b):
        first = jnp.broadcast_to(side[:, 0:128], (8, 128))
        second = jnp.broadcast_to(side[:, 128:256], (8, 128))
        lists.append(jnp.where((sub8 & 1) == 0, first, second))
    lists_out[0:8, :] = lists[0]
    lists_out[8:16, :] = lists[1]

    for c in range(3):
        for h in range(16):
            load_out[c * 16 + h : c * 16 + h + 1, :] = load_ref[c : c + 1, h * 128 : h * 128 + 128]
    load_a, load_b = halos_of(load_out[...], lists)
    a_out[0:8, :] = load_a
    b_out[0:8, :] = load_b

    row12 = iota((12, 256), 0)
    zero16 = jnp.zeros((), BF16)
    lumped = None
    for copy in large:
        copy.wait()
    for block in range(ELEMS // 256):
        for n in range(4):
            span = slice(block * 256, block * 256 + 256)
            nodes = conn_ref[n : n + 1, span]
            mask = high_mask(nodes)
            rows = []
            for j in range(3 * n, 3 * n + 3):
                column = mats_ref[j, :, span].astype(F32)
                rows.append(jnp.where(mask, bf16_rows(column[j : j + 1, :], 16), zero16))
                mats_ref[j, :, span] = jnp.where(row12 == j, 0.0, column).astype(BF16)
            piece = times_one_hot(jnp.concatenate(rows, axis=0), nodes)
            lumped = piece if lumped is None else lumped + piece
    lumped_out[...] = lumped
    lump_a, lump_b = halos_of(lumped, lists)
    a_out[8:16, :] = lump_a
    b_out[8:16, :] = lump_b


def at_corners(tables_of, index_ref, out_ref):
    for t in range(2):
        tables = tables_of(t)
        for start in range(0, ELEMS, 128):
            nodes = index_ref[8 * t : 8 * t + 8, start : start + 128]
            lanes = nodes & 127
            out_ref[8 * t : 8 * t + 8, start : start + 128] = pick([lane_take(table, lanes) for table in tables], nodes >> 7)


def component_of_row(t):
    return (iota((8, 128), 0) + 2 * t) % 3


def corner_tables(field):
    rows = [field_rows(field, block) for block in range(16)]
    return lambda t: [by_component(r, component_of_row(t)) for r in rows]


def list_kernel(conn_ref, lists_ref, index_out, inverse_out, place_out, hot_out):
    lane = iota((16, 256), 1)
    zero = jnp.zeros((), BF16)
    found = None
    for t in range(2):
        side = jnp.concatenate([lists_ref[8 * t : 8 * t + 1, :], lists_ref[8 * t + 1 : 8 * t + 2, :]], axis=1)
        mask = high_mask(side)
        place = jnp.where(mask, (lane & 127).astype(F32).astype(BF16), zero)
        code = jnp.where(mask, (2 * t + (lane >> 7) + 1).astype(F32).astype(BF16), zero)
        piece = times_one_hot(jnp.concatenate([place, code], axis=0), side)
        found = piece if found is None else found + piece
    inverse = (found[16:32].astype(jnp.int32) - 1) * 128 + found[0:16].astype(jnp.int32)
    inverse_out[...] = inverse
    for j in range(12):
        index_out[j : j + 1, :] = conn_ref[j // 3 : j // 3 + 1, :]
    index_out[12:16, :] = jnp.zeros((4, ELEMS), jnp.int32)
    tables = [jnp.broadcast_to(inverse[block : block + 1, :], (8, 128)) for block in range(16)]
    at_corners(lambda t: tables, index_out, place_out)
    lane128 = iota((128, 128), 1).astype(F32)
    for start in range(0, ELEMS, 128):
        low = (conn_ref[:, start : start + 128] & 127).astype(F32)
        columns = jnp.concatenate([low, low], axis=0).T
        for n in range(4):
            same_low = jnp.broadcast_to(columns[:, n : n + 1], (128, 128)) == lane128
            hot_out[n, start : start + 128, :] = jnp.where(same_low, 1.0, 0.0).astype(BF16)


def early_kernel(past_ref, index_ref, *rest):
    if len(rest) == 3:
        diag_ref, corner_out, scale_out = rest
        at_corners(corner_tables(1.0 / diag_ref[...]), index_ref, scale_out)
    else:
        (corner_out,) = rest
    at_corners(corner_tables(past_ref[...]), index_ref, corner_out)


def apply_off_diagonal(corner, mats_ref, conn_ref, hot_ref):
    def product(start):
        gathered = corner(start)
        out = jnp.zeros((12, 128), F32)
        for j in range(12):
            column = mats_ref[j, :, start : start + 128].astype(F32)
            value = gathered[j // 8][j % 8 : j % 8 + 1, :]
            out = out + column * jnp.broadcast_to(value, (12, 128))
        return out

    def values_of(start):
        return jnp.concatenate([product(start), product(start + 128)], axis=1)

    return scatter(values_of, conn_ref, hot_ref)


def full_corner(field, index_ref, table_ref):
    of = corner_tables(field)
    for t in range(2):
        for block, table in enumerate(of(t)):
            table_ref[block, 8 * t : 8 * t + 8, :] = table

    def corner(start):
        index = index_ref[:, start : start + 128]
        gathered = []
        for t in range(2):
            nodes = index[8 * t : 8 * t + 8]
            lanes = nodes & 127
            gathered.append(pick([lane_take(table_ref[block, 8 * t : 8 * t + 8, :], lanes) for block in range(16)], nodes >> 7))
        return gathered

    return corner


def late_corner(corner_ref, scale_ref, place_ref, near):
    tables = []
    for t in range(2):
        comp = component_of_row(t)
        tables.append([])
        for block in range(4):
            k, values = block & 1, near[block >> 1]
            rows = [jnp.broadcast_to(values[2 * c + k : 2 * c + k + 1, :], (8, 128)) for c in range(3)]
            tables[t].append(by_component(rows, comp))

    def corner(start):
        gathered = []
        for t in range(2):
            at = (slice(8 * t, 8 * t + 8), slice(start, start + 128))
            place = place_ref[at]
            lanes, code = place & 127, place >> 7
            extra = pick([lane_take(table, lanes) for table in tables[t]], code)
            gathered.append((corner_ref[at] + jnp.where(code >= 0, extra, 0.0)) * scale_ref[at])
        return gathered

    return corner


def tile_sum(product):
    out = product[0:8, :]
    for i in range(1, 6):
        out = out + product[8 * i : 8 * i + 8, :]
    return out


def step(basis, corner, lumped_ref, mats_ref, conn_ref, hot_ref, lists_ref, image_out, sums_out):
    image = apply_off_diagonal(corner, mats_ref, conn_ref, hot_ref)
    image_out[...] = image
    sums_out[0:8, :] = tile_sum(basis * basis * lumped_ref[...])
    sums_out[8:16, :] = tile_sum(basis * image)
    return halos_of(image, [lists_ref[0:8, :], lists_ref[8:16, :]])


def second_kernel(
    load_ref, lumped_ref, inverse_ref, lists_ref, index_ref, conn_ref, hot_ref, mats_ref, near_b, near_a,
    diag_out, basis_out, image_out, sums_out, a_out, b_out, table_ref,
):
    inverse = inverse_ref[...]
    force = assembled(load_ref[...], inverse, [near_a[0:8, :], near_b[0:8, :]])
    diag = assembled(lumped_ref[...], inverse, [near_a[8:16, :], near_b[8:16, :]])
    basis = force / diag
    diag_out[...] = diag
    basis_out[...] = basis
    corner = full_corner(basis, index_ref, table_ref)
    halos = step(basis, corner, lumped_ref, mats_ref, conn_ref, hot_ref, lists_ref, image_out, sums_out)
    a_out[...] = halos[0]
    b_out[...] = halos[1]


def late_step(past_ref, corner_ref, scale_ref, place_ref, diag_ref, lumped_ref, inverse_ref, lists_ref, conn_ref, hot_ref, mats_ref, near_b, near_a, basis_out, image_out, sums_out):
    near = [near_a[...], near_b[...]]
    basis = assembled(past_ref[...], inverse_ref[...], near) / diag_ref[...]
    basis_out[...] = basis
    corner = late_corner(corner_ref, scale_ref, place_ref, near)
    return step(basis, corner, lumped_ref, mats_ref, conn_ref, hot_ref, lists_ref, image_out, sums_out)


def middle_kernel(
    past_ref, corner_ref, scale_ref, place_ref, diag_ref, lumped_ref, inverse_ref, lists_ref, conn_ref, hot_ref, mats_ref, near_b, near_a,
    basis_out, image_out, sums_out, a_out, b_out,
):
    halos = late_step(
        past_ref, corner_ref, scale_ref, place_ref, diag_ref, lumped_ref, inverse_ref, lists_ref, conn_ref, hot_ref, mats_ref, near_b, near_a,
        basis_out, image_out, sums_out,
    )
    a_out[...] = halos[0]
    b_out[...] = halos[1]


def place():
    return tuple(lax.axis_index(a) for a in AXES)


def slab_slot(slab):
    return (slab // 128) * 8 + slab % 8


def fourth_kernel(
    past_ref, corner_ref, scale_ref, place_ref, diag_ref, lumped_ref, inverse_ref, lists_ref, conn_ref, hot_ref, mats_ref, near_b, near_a,
    sums0, sums1, sums2,
    basis_out, image_out, message_out, sums_ref,
):
    halos = late_step(
        past_ref, corner_ref, scale_ref, place_ref, diag_ref, lumped_ref, inverse_ref, lists_ref, conn_ref, hot_ref, mats_ref, near_b, near_a,
        basis_out, image_out, sums_ref,
    )
    lane = iota((8, 128), 1)
    sub = iota((8, 128), 0)
    moments = jnp.zeros((8, 128), F32)
    for k, ref in enumerate((sums0, sums1, sums2, sums_ref)):
        for t in range(2):
            total = jnp.sum(ref[8 * t : 8 * t + 8, :], axis=0, keepdims=True)
            total = jnp.sum(jnp.broadcast_to(total, (8, 128)), axis=1, keepdims=True)
            moments = jnp.where(lane == 2 * k + t, total, moments)
    moments = jnp.where(sub == 6, moments, 0.0)
    message_out[...] = jnp.broadcast_to(moments[None], (32, 8, 128))
    x, z, y, c = place()
    slab = ((x * 16 + z) * 4 + y) * 2 + c
    odd = c == 1
    to_right = jnp.where(sub < 6, jnp.where(odd, halos[1], halos[0]), moments)
    to_left = jnp.where(sub < 6, jnp.where(odd, halos[0], halos[1]), moments)

    @pl.when(slab < 511)
    def _():
        message_out[slab_slot(jnp.minimum(slab + 1, 511))] = to_right

    @pl.when(slab > 0)
    def _():
        message_out[slab_slot(jnp.maximum(slab - 1, 0))] = to_left


def relay_kernel(message_ref, message_out, direct_out):
    x, z, y, c = place()
    slot = x * 8 + y * 2 + c
    first = (y == 0) & (c == 0)
    last = (y == 3) & (c == 1)
    sub = iota((8, 128), 0)
    moments = message_ref[0]
    for i in range(1, 32):
        moments = moments + message_ref[i]
    moments = jnp.where(sub == 6, moments, 0.0)
    message_out[...] = jnp.broadcast_to(moments[None], (16, 8, 128))
    source_r = jnp.where(first, jnp.where(z < 15, x * 8 + 7, jnp.maximum(x * 8 - 1, 0)), jnp.maximum(slot - 1, 0))
    source_l = jnp.where(last, jnp.where(z > 0, x * 8, jnp.minimum(x * 8 + 8, 31)), jnp.minimum(slot + 1, 31))
    from_left = message_ref[source_r]
    from_right = message_ref[source_l]
    direct_out[0:8, :] = from_left
    direct_out[8:16, :] = from_right

    @pl.when(first)
    def _():
        message_out[(z + 1) % 16] = jnp.where(sub < 6, from_left, moments)

    @pl.when(last)
    def _():
        message_out[(z + 15) % 16] = jnp.where(sub < 6, from_right, moments)


def coefficients(moment):
    zero, one = jnp.zeros((8, 128), F32), jnp.ones((8, 128), F32)
    scale = [jnp.where(moment[2 * i] > 0.0, lax.rsqrt(jnp.where(moment[2 * i] > 0.0, moment[2 * i], one)), zero) for i in range(4)]
    rows = [[moment[i + j] * scale[i] * scale[j] for j in range(4)] + [-moment[i + 4] * scale[i]] for i in range(4)]
    least = one
    inverse = []
    for i in range(4):
        pivot = rows[i][i]
        good = pivot > 1e-6
        least = jnp.minimum(least, jnp.where(good, pivot, zero))
        inverse.append(jnp.where(good, one / jnp.where(good, pivot, one), zero))
        for j in range(i + 1, 4):
            ratio = rows[j][i] * inverse[i]
            for k in range(i + 1, 5):
                rows[j][k] = rows[j][k] - ratio * rows[i][k]
    coef = [zero] * 4
    for i in (3, 2, 1, 0):
        total = rows[i][4]
        for j in range(i + 1, 4):
            total = total - rows[i][j] * coef[j]
        coef[i] = total * inverse[i]
    coef = [coef[i] * scale[i] for i in range(4)]
    at = coef[0] - coef[1] + coef[2] - coef[3] + one
    resid = [v / at for v in coef] + [one / at]
    accel = [None] * 4
    accel[3] = -resid[4]
    for i in (2, 1, 0):
        accel[i] = -resid[i + 1] - accel[i + 1]
    good = (least > PIVOT_FLOOR) & (at > 0.0)
    return accel, resid, good


def last_kernel(message_ref, direct_ref, image_ref, diag_ref, inverse_ref, b0, b1, b2, b3, accel_out, resid_out, flag_out):
    x, z, y, c = place()
    slab = ((x * 16 + z) * 4 + y) * 2 + c
    first = (y == 0) & (c == 0)
    last = (y == 3) & (c == 1)
    lane = iota((8, 128), 1)
    total = message_ref[0]
    for i in range(1, 16):
        total = total + message_ref[i]
    total = jnp.broadcast_to(total[6:7, :], (8, 128))
    moment = [
        jnp.broadcast_to(jnp.sum(jnp.where(lane == k, total, 0.0), axis=1, keepdims=True), (8, 128)) for k in range(8)
    ]
    accel_coef, resid_coef, good = coefficients(moment)
    from_left = jnp.where(first, message_ref[(z + 15) % 16], direct_ref[0:8, :])
    from_right = jnp.where(last, message_ref[(z + 1) % 16], direct_ref[8:16, :])
    from_left = jnp.where(slab > 0, from_left, 0.0)
    from_right = jnp.where(slab < 511, from_right, 0.0)
    odd = c == 1
    near = [jnp.where(odd, from_left, from_right), jnp.where(odd, from_right, from_left)]
    diag = diag_ref[...]
    image = assembled(image_ref[...], inverse_ref[...], near)
    for c_ in range(3):
        for half in range(2):
            rows = slice(c_ * 16 + half * 8, c_ * 16 + half * 8 + 8)
            basis = [r[rows, :] for r in (b0, b1, b2, b3)]
            accel = basis[3] * accel_coef[3]
            part = basis[3] * resid_coef[3]
            for k in (2, 1, 0):
                accel = accel + basis[k] * accel_coef[k]
                part = part + basis[k] * resid_coef[k]
            resid = image[rows, :] * resid_coef[4] + diag[rows, :] * part
            for h in range(8):
                start = (half * 8 + h) * 128
                accel_out[c_ : c_ + 1, start : start + 128] = accel[h : h + 1, :]
                resid_out[c_ : c_ + 1, start : start + 128] = resid[h : h + 1, :]
    flag_out[0, 0] = jnp.min(jnp.where(good, 1, 0))


def call(kernel, outs, *args, scratch=(), smem_out=None, space=pltpu.VMEM, work=None):
    out_specs = [pl.BlockSpec(memory_space=pltpu.VMEM)] * len(outs)
    if smem_out is not None:
        out_specs[smem_out] = pl.BlockSpec(memory_space=pltpu.SMEM)
    return pl.pallas_call(
        kernel,
        out_shape=[jax.ShapeDtypeStruct(s, t) for s, t in outs],
        in_specs=[pl.BlockSpec(memory_space=space)] * len(args),
        out_specs=out_specs,
        scratch_shapes=list(scratch),
        compiler_params=pltpu.CompilerParams(vmem_limit_bytes=VMEM_LIMIT),
        cost_estimate=work,
    )(*args)


def same(*args):
    def kernel(*refs):
        for src, dst in zip(refs[: len(args)], refs[len(args) :]):
            dst[...] = src[...]

    return call(kernel, [(a.shape, a.dtype) for a in args], *args)


def swap(side_a, side_b):
    count = 512
    from_b = lax.ppermute(side_b, AXES, [(i, ((i + 1) ^ 1) - 1) for i in range(1, count - 1)])
    from_a = lax.ppermute(side_a, AXES, [(i, i ^ 1) for i in range(count)])
    return from_a, from_b


def plain(load, element_mats, connect, shared):
    node_count = load.shape[1]
    slab_index = lax.axis_index(AXES)
    slab_count = 512
    left_weight = jnp.where(slab_index > 0, F32(0.5), F32(1.0))
    right_weight = jnp.where(slab_index < slab_count - 1, F32(0.5), F32(1.0))
    weights = jnp.ones((node_count,), F32).at[shared[0]].set(left_weight).at[shared[1]].set(right_weight)

    def inner(first, second):
        return lax.psum(jnp.sum(weights * jnp.sum(first * second, axis=0)), AXES)

    def assemble(partial_value):
        from_left = lax.ppermute(partial_value[:, shared[1]], AXES, [(i, i + 1) for i in range(slab_count - 1)])
        from_right = lax.ppermute(partial_value[:, shared[0]], AXES, [(i + 1, i) for i in range(slab_count - 1)])
        return partial_value.at[:, shared[0]].add(from_left).at[:, shared[1]].add(from_right)

    def spread(values):
        values = values.reshape(4, 3, -1).transpose(1, 0, 2).reshape(3, -1)
        return jnp.zeros((3, node_count), F32).at[:, connect.reshape(-1)].add(values)

    def element_apply(field):
        gathered = field[:, connect].transpose(1, 0, 2).reshape(12, -1)
        result = element_mats[:, 0, :].astype(F32) * gathered[0]
        for column in range(1, 12):
            result = result + element_mats[:, column, :].astype(F32) * gathered[column]
        return spread(result)

    lumped = spread(jnp.stack([element_mats[i, i, :].astype(F32) for i in range(12)]))
    both = assemble(jnp.concatenate([load, lumped], axis=0))
    residual, diagonal = both[:3], both[3:]
    direction = residual / diagonal
    accel = jnp.zeros_like(residual)
    gamma = inner(residual, direction)

    def body(_, carry):
        accel, residual, direction, gamma = carry
        image = assemble(element_apply(direction))
        alpha = gamma / inner(direction, image)
        accel = accel + alpha * direction
        residual = residual - alpha * image
        precond = residual / diagonal
        following = inner(residual, precond)
        return accel, residual, precond + following / gamma * direction, following

    accel, residual, _, _ = lax.fori_loop(0, ITERS, body, (accel, residual, direction, gamma))
    return accel, residual


def body(load, element_mats, connect, shared):
    field = ((48, 128), F32)
    halo = ((8, 128), F32)
    sums = ((16, 128), F32)
    corners = ((16, ELEMS), F32)
    index = ((16, ELEMS), jnp.int32)
    inverse = ((16, 128), jnp.int32)
    load_f, lumped, mats, conn, lists, a, b = call(
        first_kernel,
        [field, field, ((12, 12, ELEMS), BF16), ((4, ELEMS), jnp.int32), inverse, sums, sums],
        load, element_mats, connect, shared,
        scratch=[pltpu.VMEM((3, NODES), F32), pltpu.VMEM((2, SHARED), jnp.int32), pltpu.SemaphoreType.DMA((15,))],
        space=pltpu.HBM,
    )
    a, b = swap(a, b)
    index, inverse, places, hot = call(
        list_kernel, [index, inverse, index, ((4, ELEMS, 128), BF16)], conn, lists, work=EARLY_WORK
    )
    diag, b0, image, total, a, b = call(
        second_kernel,
        [field, field, field, sums, halo, halo],
        load_f, lumped, inverse, lists, index, conn, hot, mats, b, a,
        scratch=[pltpu.VMEM((16, 16, 128), F32)],
    )
    bases, totals = [b0], [total]
    for round_ in range(3):
        a, b = swap(a, b)
        if round_ == 0:
            corner, scale = call(early_kernel, [corners, corners], image, index, diag, work=EARLY_WORK)
        else:
            (corner,) = call(early_kernel, [corners], image, index, work=EARLY_WORK)
        args = (image, corner, scale, places, diag, lumped, inverse, lists, conn, hot, mats, b, a)
        if round_ < 2:
            basis, image, total, a, b = call(middle_kernel, [field, field, sums, halo, halo], *args)
            bases.append(basis)
            totals.append(total)
    basis, image, message = call(
        fourth_kernel,
        [field, field, ((32, 8, 128), F32)],
        *args, *totals,
        scratch=[pltpu.VMEM((16, 128), F32)],
    )
    bases.append(basis)
    message = lax.all_to_all(message, GROUP, 0, 0, tiled=True)
    message, direct = call(relay_kernel, [((16, 8, 128), F32), sums], message)
    message = lax.all_to_all(message, "z", 0, 0, tiled=True)
    accel, residual, flag = call(
        last_kernel,
        [((3, NODES), F32), ((3, NODES), F32), ((1, 1), jnp.int32)],
        message, direct, image, diag, inverse, *bases,
        smem_out=2,
    )

    def again(carry):
        args = same(load, element_mats, connect, shared)
        return (jnp.int32(1),) + tuple(same(*plain(*args)))

    _, accel, residual = lax.while_loop(lambda carry: carry[0] == 0, again, (flag.reshape(()), accel, residual))
    return accel, residual


def solution(mesh):
    parts = Mesh(mesh.devices.reshape(4, 16, 4, 2), AXES)
    return jax.shard_map(
        body,
        mesh=parts,
        in_specs=(P(None, AXES), P(None, None, AXES), P(None, AXES), P(None, AXES)),
        out_specs=(P(None, AXES), P(None, AXES)),
        check_vma=False,
    )
```

```python
import jax
import jax.numpy as jnp
from jax import lax
from jax.experimental import pallas as pl
from jax.experimental.pallas import tpu as pltpu
from jax.sharding import Mesh, PartitionSpec as P

ITERS = 4
AXES = ("x", "z", "y", "c")
GROUP = ("x", "y", "c")
NODES = 2048
ELEMS = 2048
SHARED = 256
SPLITS = 3
PIVOT_FLOOR = 0.02
F32 = jnp.float32
BF16 = jnp.bfloat16
EARLY_WORK = pl.CostEstimate(flops=2_000_000, bytes_accessed=400_000, transcendentals=0)
VMEM_LIMIT = 32 * 1024 * 1024


def iota(shape, dim):
    return lax.broadcasted_iota(jnp.int32, shape, dim)


def lane_take(table, lanes):
    return jnp.take_along_axis(table, lanes, axis=1, mode="promise_in_bounds")


def pick(parts, high):
    bit = 0
    while len(parts) > 1:
        odd = (high & (1 << bit)) != 0
        parts = [jnp.where(odd, parts[i + 1], parts[i]) for i in range(0, len(parts), 2)]
        bit += 1
    return parts[0]


def field_rows(field, block):
    return [jnp.broadcast_to(field[c * 16 + block : c * 16 + block + 1, :], (8, 128)) for c in range(3)]


def by_component(rows, comp):
    return jnp.where(comp == 0, rows[0], jnp.where(comp == 1, rows[1], rows[2]))


def halos_of(field, lists):
    comp = iota((8, 128), 0) // 2
    tables = [by_component(field_rows(field, block), comp) for block in range(16)]
    out = []
    for nodes in lists:
        out.append(pick([lane_take(t, nodes & 127) for t in tables], nodes >> 7))
    return out


def assembled(field, inverse, near, blocks=range(4)):
    tiles = []
    for c in range(3):
        for half in range(2):
            place = inverse[half * 8 : half * 8 + 8, :]
            lanes, code = place & 127, place >> 7
            parts = []
            for t in blocks:
                row = 2 * c + (t & 1)
                table = jnp.broadcast_to(near[t >> 1][row : row + 1, :], (8, 128))
                parts.append(lane_take(table, lanes))
            start = c * 16 + half * 8
            here = (code >= blocks[0]) & (code <= blocks[-1])
            tiles.append(field[start : start + 8, :] + jnp.where(here, pick(parts, code), 0.0))
    return jnp.concatenate(tiles, axis=0)


def bf16_rows(row, count):
    return jnp.broadcast_to(row.astype(F32), (count, row.shape[1])).astype(BF16)


def bf16_iota(shape):
    return iota(shape, 0).astype(F32).astype(BF16)


def high_mask(nodes):
    return bf16_rows(nodes >> 7, 16) == bf16_iota((16, nodes.shape[1]))


def corner_lhs(values, conn):
    zero = jnp.zeros((), BF16)
    parts = []
    rest = values
    for _ in range(SPLITS - 1):
        top = rest.astype(BF16).astype(F32)
        parts.append(top)
        rest = rest - top
    parts.append(rest)
    out = []
    for n in range(4):
        mask = high_mask(conn[n : n + 1, :])
        rows = [part[3 * n + c : 3 * n + c + 1, :] for part in parts for c in range(3)]
        out.append(jnp.concatenate([jnp.where(mask, bf16_rows(row, 16), zero) for row in rows], axis=0))
    return out


def times_one_hot(lhs, nodes):
    shape = (128, nodes.shape[1])
    hot = jnp.where(bf16_rows(nodes & 127, 128) == bf16_iota(shape), jnp.ones((), BF16), jnp.zeros((), BF16))
    return lax.dot_general(lhs, hot, (((1,), (1,)), ((), ())), preferred_element_type=F32)


def scatter(values_of, conn_ref):
    total = None
    for block in range(ELEMS // 256):
        start = block * 256
        conn = conn_ref[:, start : start + 256]
        lhs = corner_lhs(values_of(start), conn)
        for n in range(4):
            piece = times_one_hot(lhs[n], conn[n : n + 1, :])
            total = piece if total is None else total + piece
    out = total[0:48]
    for t in range(1, SPLITS):
        out = out + total[48 * t : 48 * t + 48]
    return out


def first_kernel(
    load_hbm, mats_hbm, conn_hbm, shared_hbm,
    load_out, lumped_out, mats_ref, conn_ref, lists_out, a_out, b_out,
    load_ref, shared_ref, sems,
):
    small = [
        pltpu.make_async_copy(shared_hbm, shared_ref, sems.at[0]),
        pltpu.make_async_copy(conn_hbm, conn_ref, sems.at[1]),
        pltpu.make_async_copy(load_hbm, load_ref, sems.at[2]),
    ]
    large = [
        pltpu.make_async_copy(mats_hbm.at[pl.ds(3 * i, 3)], mats_ref.at[pl.ds(3 * i, 3)], sems.at[3 + i]) for i in range(4)
    ]
    for copy in small[:2] + large + small[2:]:
        copy.start()
    for copy in small + large:
        copy.wait()
    odd = lax.axis_index("c") == 1
    own = shared_ref[...]
    row0, row1 = own[0:1, :], own[1:2, :]
    side_a = jnp.where(odd, row0, row1)
    side_b = jnp.where(odd, row1, row0)

    sub8 = iota((8, 128), 0)
    lists = []
    for side in (side_a, side_b):
        first = jnp.broadcast_to(side[:, 0:128], (8, 128))
        second = jnp.broadcast_to(side[:, 128:256], (8, 128))
        lists.append(jnp.where((sub8 & 1) == 0, first, second))
    lists_out[0:8, :] = lists[0]
    lists_out[8:16, :] = lists[1]

    for c in range(3):
        for h in range(16):
            load_out[c * 16 + h : c * 16 + h + 1, :] = load_ref[c : c + 1, h * 128 : h * 128 + 128]
    load_a, load_b = halos_of(load_out[...], lists)
    a_out[0:8, :] = load_a
    b_out[0:8, :] = load_b

    row12 = iota((12, 256), 0)
    zero16 = jnp.zeros((), BF16)
    lumped = None
    for block in range(ELEMS // 256):
        for n in range(4):
            span = slice(block * 256, block * 256 + 256)
            nodes = conn_ref[n : n + 1, span]
            mask = high_mask(nodes)
            rows = []
            for j in range(3 * n, 3 * n + 3):
                column = mats_ref[j, :, span].astype(F32)
                rows.append(jnp.where(mask, bf16_rows(column[j : j + 1, :], 16), zero16))
                mats_ref[j, :, span] = jnp.where(row12 == j, 0.0, column).astype(BF16)
            low = jnp.where(bf16_rows(nodes & 127, 128) == bf16_iota((128, 256)), jnp.ones((), BF16), zero16)
            piece = lax.dot_general(low, jnp.concatenate(rows, axis=0), (((1,), (1,)), ((), ())), preferred_element_type=F32)
            lumped = piece if lumped is None else lumped + piece
    lumped = lumped.T
    lumped_out[...] = lumped
    lump_a, lump_b = halos_of(lumped, lists)
    a_out[8:16, :] = lump_a
    b_out[8:16, :] = lump_b


def at_corners(tables_of, index_ref, out_ref):
    for t in range(2):
        tables = tables_of(t)
        for start in range(0, ELEMS, 128):
            nodes = index_ref[8 * t : 8 * t + 8, start : start + 128]
            lanes = nodes & 127
            out_ref[8 * t : 8 * t + 8, start : start + 128] = pick([lane_take(table, lanes) for table in tables], nodes >> 7)


def component_of_row(t):
    return (iota((8, 128), 0) + 2 * t) % 3


def corner_tables(field):
    rows = [field_rows(field, block) for block in range(16)]
    return lambda t: [by_component(r, component_of_row(t)) for r in rows]


def list_kernel(conn_ref, lists_ref, index_out, inverse_out, place_out):
    lane = iota((16, 256), 1)
    zero = jnp.zeros((), BF16)
    found = None
    for t in range(2):
        side = jnp.concatenate([lists_ref[8 * t : 8 * t + 1, :], lists_ref[8 * t + 1 : 8 * t + 2, :]], axis=1)
        mask = high_mask(side)
        place = jnp.where(mask, (lane & 127).astype(F32).astype(BF16), zero)
        code = jnp.where(mask, (2 * t + (lane >> 7) + 1).astype(F32).astype(BF16), zero)
        piece = times_one_hot(jnp.concatenate([place, code], axis=0), side)
        found = piece if found is None else found + piece
    inverse = (found[16:32].astype(jnp.int32) - 1) * 128 + found[0:16].astype(jnp.int32)
    inverse_out[...] = inverse
    for j in range(12):
        index_out[j : j + 1, :] = conn_ref[j // 3 : j // 3 + 1, :]
    index_out[12:16, :] = jnp.zeros((4, ELEMS), jnp.int32)
    tables = [jnp.broadcast_to(inverse[block : block + 1, :], (8, 128)) for block in range(16)]
    at_corners(lambda t: tables, index_out, place_out)


def early_kernel(past_ref, index_ref, *rest):
    if len(rest) == 3:
        diag_ref, corner_out, scale_out = rest
        at_corners(corner_tables(1.0 / diag_ref[...]), index_ref, scale_out)
    else:
        (corner_out,) = rest
    at_corners(corner_tables(past_ref[...]), index_ref, corner_out)


def apply_off_diagonal(corner, mats_ref, conn_ref):
    def product(start):
        gathered = corner(start)
        out = jnp.zeros((12, 128), F32)
        for j in range(12):
            column = mats_ref[j, :, start : start + 128].astype(F32)
            value = gathered[j // 8][j % 8 : j % 8 + 1, :]
            out = out + column * jnp.broadcast_to(value, (12, 128))
        return out

    def values_of(start):
        return jnp.concatenate([product(start), product(start + 128)], axis=1)

    return scatter(values_of, conn_ref)


def full_corner(field, index_ref, table_ref):
    of = corner_tables(field)
    for t in range(2):
        for block, table in enumerate(of(t)):
            table_ref[block, 8 * t : 8 * t + 8, :] = table

    def corner(start):
        index = index_ref[:, start : start + 128]
        gathered = []
        for t in range(2):
            nodes = index[8 * t : 8 * t + 8]
            lanes = nodes & 127
            gathered.append(pick([lane_take(table_ref[block, 8 * t : 8 * t + 8, :], lanes) for block in range(16)], nodes >> 7))
        return gathered

    return corner


def late_corner(corner_ref, scale_ref, place_ref, near):
    tables = []
    for t in range(2):
        comp = component_of_row(t)
        tables.append([])
        for block in range(4):
            k, values = block & 1, near[block >> 1]
            rows = [jnp.broadcast_to(values[2 * c + k : 2 * c + k + 1, :], (8, 128)) for c in range(3)]
            tables[t].append(by_component(rows, comp))

    def corner(start):
        gathered = []
        for t in range(2):
            at = (slice(8 * t, 8 * t + 8), slice(start, start + 128))
            place = place_ref[at]
            lanes, code = place & 127, place >> 7
            extra = pick([lane_take(table, lanes) for table in tables[t]], code)
            gathered.append((corner_ref[at] + jnp.where(code >= 0, extra, 0.0)) * scale_ref[at])
        return gathered

    return corner


def tile_sum(product):
    out = product[0:8, :]
    for i in range(1, 6):
        out = out + product[8 * i : 8 * i + 8, :]
    return out


def step(basis, corner, lumped_ref, mats_ref, conn_ref, lists_ref, image_out, sums_out):
    image = apply_off_diagonal(corner, mats_ref, conn_ref)
    image_out[...] = image
    sums_out[0:8, :] = tile_sum(basis * basis * lumped_ref[...])
    sums_out[8:16, :] = tile_sum(basis * image)
    return halos_of(image, [lists_ref[0:8, :], lists_ref[8:16, :]])


def second_kernel(
    load_ref, lumped_ref, inverse_ref, lists_ref, index_ref, conn_ref, mats_ref, near_b, near_a,
    diag_out, basis_out, image_out, sums_out, a_out, b_out, table_ref,
):
    inverse = inverse_ref[...]
    force = assembled(load_ref[...], inverse, [near_a[0:8, :], near_b[0:8, :]])
    diag = assembled(lumped_ref[...], inverse, [near_a[8:16, :], near_b[8:16, :]])
    basis = force / diag
    diag_out[...] = diag
    basis_out[...] = basis
    corner = full_corner(basis, index_ref, table_ref)
    halos = step(basis, corner, lumped_ref, mats_ref, conn_ref, lists_ref, image_out, sums_out)
    a_out[...] = halos[0]
    b_out[...] = halos[1]


def late_step(past_ref, corner_ref, scale_ref, place_ref, diag_ref, lumped_ref, inverse_ref, lists_ref, conn_ref, mats_ref, near_b, near_a, basis_out, image_out, sums_out):
    near = [near_a[...], near_b[...]]
    basis = assembled(past_ref[...], inverse_ref[...], near) / diag_ref[...]
    basis_out[...] = basis
    corner = late_corner(corner_ref, scale_ref, place_ref, near)
    return step(basis, corner, lumped_ref, mats_ref, conn_ref, lists_ref, image_out, sums_out)


def middle_kernel(
    past_ref, corner_ref, scale_ref, place_ref, diag_ref, lumped_ref, inverse_ref, lists_ref, conn_ref, mats_ref, near_b, near_a,
    basis_out, image_out, sums_out, a_out, b_out,
):
    halos = late_step(
        past_ref, corner_ref, scale_ref, place_ref, diag_ref, lumped_ref, inverse_ref, lists_ref, conn_ref, mats_ref, near_b, near_a,
        basis_out, image_out, sums_out,
    )
    a_out[...] = halos[0]
    b_out[...] = halos[1]


def place():
    return tuple(lax.axis_index(a) for a in AXES)


def fourth_kernel(
    past_ref, corner_ref, scale_ref, place_ref, diag_ref, lumped_ref, inverse_ref, lists_ref, conn_ref, mats_ref, near_b, near_a,
    sums0, sums1, sums2,
    basis_out, image_out, message_out, own_out, sums_ref,
):
    halos = late_step(
        past_ref, corner_ref, scale_ref, place_ref, diag_ref, lumped_ref, inverse_ref, lists_ref, conn_ref, mats_ref, near_b, near_a,
        basis_out, image_out, sums_ref,
    )
    lane = iota((8, 128), 1)
    sub = iota((8, 128), 0)
    moments = jnp.zeros((8, 128), F32)
    for k, ref in enumerate((sums0, sums1, sums2, sums_ref)):
        for t in range(2):
            total = jnp.sum(ref[8 * t : 8 * t + 8, :], axis=0, keepdims=True)
            total = jnp.sum(jnp.broadcast_to(total, (8, 128)), axis=1, keepdims=True)
            moments = jnp.where(lane == 2 * k + t, total, moments)
    moments = jnp.where(sub == 6, moments, 0.0)
    message_out[...] = jnp.broadcast_to(moments[None], (16, 8, 128))
    x, z, y, c = place()
    odd = c == 1
    to_right = jnp.where(odd, halos[1], halos[0])
    to_left = jnp.where(odd, halos[0], halos[1])
    own_out[0:8, :] = to_right
    own_out[8:16, :] = to_left

    @pl.when((y == 3) & (c == 1))
    def _():
        message_out[(z + 1) % 16] = jnp.where(sub < 6, to_right, moments)

    @pl.when((y == 0) & (c == 0))
    def _():
        message_out[(z + 15) % 16] = jnp.where(sub < 6, to_left, moments)


def neighbour_slots():
    x, z, y, c = place()
    slot = x * 8 + y * 2 + c
    first = (y == 0) & (c == 0)
    last = (y == 3) & (c == 1)
    before = jnp.where(first, jnp.where(z > 0, x * 8 + 7, x * 8 - 1), slot - 1)
    after = jnp.where(last, jnp.where(z < 15, x * 8, x * 8 + 8), slot + 1)
    return before, after


def relay_kernel(message_ref, own_ref, message_out):
    x, z, y, c = place()
    slot = x * 8 + y * 2 + c
    first = (y == 0) & (c == 0)
    last = (y == 3) & (c == 1)
    sub = iota((8, 128), 0)
    moments = message_ref[0]
    for i in range(1, 16):
        moments = moments + message_ref[i]
    moments = jnp.where(sub == 6, moments, 0.0)
    message_out[...] = jnp.broadcast_to(moments[None], (32, 8, 128))
    to_right = jnp.where(last, message_ref[(z + 15) % 16], own_ref[0:8, :])
    to_left = jnp.where(first, message_ref[(z + 1) % 16], own_ref[8:16, :])
    right = jnp.where(last, jnp.where(z > 0, x * 8, x * 8 + 8), slot + 1)
    left = jnp.where(first, jnp.where(z < 15, x * 8 + 7, x * 8 - 1), slot - 1)

    @pl.when(right < 32)
    def _():
        message_out[jnp.minimum(right, 31)] = jnp.where(sub < 6, to_right, moments)

    @pl.when(left >= 0)
    def _():
        message_out[jnp.maximum(left, 0)] = jnp.where(sub < 6, to_left, moments)


def coefficients(moment):
    zero, one = jnp.zeros((8, 128), F32), jnp.ones((8, 128), F32)
    scale = [jnp.where(moment[2 * i] > 0.0, lax.rsqrt(jnp.where(moment[2 * i] > 0.0, moment[2 * i], one)), zero) for i in range(4)]
    rows = [[moment[i + j] * scale[i] * scale[j] for j in range(4)] + [-moment[i + 4] * scale[i]] for i in range(4)]
    least = one
    inverse = []
    for i in range(4):
        pivot = rows[i][i]
        good = pivot > 1e-6
        least = jnp.minimum(least, jnp.where(good, pivot, zero))
        inverse.append(jnp.where(good, one / jnp.where(good, pivot, one), zero))
        for j in range(i + 1, 4):
            ratio = rows[j][i] * inverse[i]
            for k in range(i + 1, 5):
                rows[j][k] = rows[j][k] - ratio * rows[i][k]
    coef = [zero] * 4
    for i in (3, 2, 1, 0):
        total = rows[i][4]
        for j in range(i + 1, 4):
            total = total - rows[i][j] * coef[j]
        coef[i] = total * inverse[i]
    coef = [coef[i] * scale[i] for i in range(4)]
    at = coef[0] - coef[1] + coef[2] - coef[3] + one
    resid = [v / at for v in coef] + [one / at]
    accel = [None] * 4
    accel[3] = -resid[4]
    for i in (2, 1, 0):
        accel[i] = -resid[i + 1] - accel[i + 1]
    good = (least > PIVOT_FLOOR) & (at > 0.0)
    return accel, resid, good


def last_kernel(message_ref, image_ref, diag_ref, inverse_ref, b0, b1, b2, b3, accel_out, resid_out, flag_out):
    before, after = neighbour_slots()
    odd = lax.axis_index("c") == 1
    lane = iota((8, 128), 1)
    total = message_ref[0]
    for i in range(1, 32):
        total = total + message_ref[i]
    total = jnp.broadcast_to(total[6:7, :], (8, 128))
    moment = [
        jnp.broadcast_to(jnp.sum(jnp.where(lane == k, total, 0.0), axis=1, keepdims=True), (8, 128)) for k in range(8)
    ]
    accel_coef, resid_coef, good = coefficients(moment)
    from_left = jnp.where(before >= 0, message_ref[jnp.maximum(before, 0)], 0.0)
    from_right = jnp.where(after < 32, message_ref[jnp.minimum(after, 31)], 0.0)
    near = [jnp.where(odd, from_left, from_right), jnp.where(odd, from_right, from_left)]
    diag = diag_ref[...]
    image = assembled(image_ref[...], inverse_ref[...], near)
    for c_ in range(3):
        for half in range(2):
            rows = slice(c_ * 16 + half * 8, c_ * 16 + half * 8 + 8)
            basis = [r[rows, :] for r in (b0, b1, b2, b3)]
            accel = basis[3] * accel_coef[3]
            part = basis[3] * resid_coef[3]
            for k in (2, 1, 0):
                accel = accel + basis[k] * accel_coef[k]
                part = part + basis[k] * resid_coef[k]
            resid = image[rows, :] * resid_coef[4] + diag[rows, :] * part
            for h in range(8):
                start = (half * 8 + h) * 128
                accel_out[c_ : c_ + 1, start : start + 128] = accel[h : h + 1, :]
                resid_out[c_ : c_ + 1, start : start + 128] = resid[h : h + 1, :]
    flag_out[0, 0] = jnp.min(jnp.where(good, 1, 0))


def call(kernel, outs, *args, scratch=(), smem_out=None, space=pltpu.VMEM, work=None):
    out_specs = [pl.BlockSpec(memory_space=pltpu.VMEM)] * len(outs)
    if smem_out is not None:
        out_specs[smem_out] = pl.BlockSpec(memory_space=pltpu.SMEM)
    return pl.pallas_call(
        kernel,
        out_shape=[jax.ShapeDtypeStruct(s, t) for s, t in outs],
        in_specs=[pl.BlockSpec(memory_space=space)] * len(args),
        out_specs=out_specs,
        scratch_shapes=list(scratch),
        compiler_params=pltpu.CompilerParams(vmem_limit_bytes=VMEM_LIMIT),
        cost_estimate=work,
    )(*args)


def same(*args):
    def kernel(*refs):
        for src, dst in zip(refs[: len(args)], refs[len(args) :]):
            dst[...] = src[...]

    return call(kernel, [(a.shape, a.dtype) for a in args], *args)


def swap(side_a, side_b):
    count = 512
    from_b = lax.ppermute(side_b, AXES, [(i, ((i + 1) ^ 1) - 1) for i in range(1, count - 1)])
    from_a = lax.ppermute(side_a, AXES, [(i, i ^ 1) for i in range(count)])
    return from_a, from_b


def plain(load, element_mats, connect, shared):
    node_count = load.shape[1]
    slab_index = lax.axis_index(AXES)
    slab_count = 512
    left_weight = jnp.where(slab_index > 0, F32(0.5), F32(1.0))
    right_weight = jnp.where(slab_index < slab_count - 1, F32(0.5), F32(1.0))
    weights = jnp.ones((node_count,), F32).at[shared[0]].set(left_weight).at[shared[1]].set(right_weight)

    def inner(first, second):
        return lax.psum(jnp.sum(weights * jnp.sum(first * second, axis=0)), AXES)

    def assemble(partial_value):
        from_left = lax.ppermute(partial_value[:, shared[1]], AXES, [(i, i + 1) for i in range(slab_count - 1)])
        from_right = lax.ppermute(partial_value[:, shared[0]], AXES, [(i + 1, i) for i in range(slab_count - 1)])
        return partial_value.at[:, shared[0]].add(from_left).at[:, shared[1]].add(from_right)

    def spread(values):
        values = values.reshape(4, 3, -1).transpose(1, 0, 2).reshape(3, -1)
        return jnp.zeros((3, node_count), F32).at[:, connect.reshape(-1)].add(values)

    def element_apply(field):
        gathered = field[:, connect].transpose(1, 0, 2).reshape(12, -1)
        result = element_mats[:, 0, :].astype(F32) * gathered[0]
        for column in range(1, 12):
            result = result + element_mats[:, column, :].astype(F32) * gathered[column]
        return spread(result)

    lumped = spread(jnp.stack([element_mats[i, i, :].astype(F32) for i in range(12)]))
    both = assemble(jnp.concatenate([load, lumped], axis=0))
    residual, diagonal = both[:3], both[3:]
    direction = residual / diagonal
    accel = jnp.zeros_like(residual)
    gamma = inner(residual, direction)

    def body(_, carry):
        accel, residual, direction, gamma = carry
        image = assemble(element_apply(direction))
        alpha = gamma / inner(direction, image)
        accel = accel + alpha * direction
        residual = residual - alpha * image
        precond = residual / diagonal
        following = inner(residual, precond)
        return accel, residual, precond + following / gamma * direction, following

    accel, residual, _, _ = lax.fori_loop(0, ITERS, body, (accel, residual, direction, gamma))
    return accel, residual


def body(load, element_mats, connect, shared):
    field = ((48, 128), F32)
    halo = ((8, 128), F32)
    sums = ((16, 128), F32)
    corners = ((16, ELEMS), F32)
    index = ((16, ELEMS), jnp.int32)
    inverse = ((16, 128), jnp.int32)
    load_f, lumped, mats, conn, lists, a, b = call(
        first_kernel,
        [field, field, ((12, 12, ELEMS), BF16), ((4, ELEMS), jnp.int32), inverse, sums, sums],
        load, element_mats, connect, shared,
        scratch=[pltpu.VMEM((3, NODES), F32), pltpu.VMEM((2, SHARED), jnp.int32), pltpu.SemaphoreType.DMA((7,))],
        space=pltpu.HBM,
    )
    a, b = swap(a, b)
    index, inverse, places = call(list_kernel, [index, inverse, index], conn, lists, work=EARLY_WORK)
    diag, b0, image, total, a, b = call(
        second_kernel,
        [field, field, field, sums, halo, halo],
        load_f, lumped, inverse, lists, index, conn, mats, b, a,
        scratch=[pltpu.VMEM((16, 16, 128), F32)],
    )
    bases, totals = [b0], [total]
    for round_ in range(3):
        a, b = swap(a, b)
        if round_ == 0:
            corner, scale = call(early_kernel, [corners, corners], image, index, diag, work=EARLY_WORK)
        else:
            (corner,) = call(early_kernel, [corners], image, index, work=EARLY_WORK)
        args = (image, corner, scale, places, diag, lumped, inverse, lists, conn, mats, b, a)
        if round_ < 2:
            basis, image, total, a, b = call(middle_kernel, [field, field, sums, halo, halo], *args)
            bases.append(basis)
            totals.append(total)
    basis, image, message, own = call(
        fourth_kernel,
        [field, field, ((16, 8, 128), F32), sums],
        *args, *totals,
        scratch=[pltpu.VMEM((16, 128), F32)],
    )
    bases.append(basis)
    message = lax.all_to_all(message, "z", 0, 0, tiled=True)
    (message,) = call(relay_kernel, [((32, 8, 128), F32)], message, own)
    message = lax.all_to_all(message, GROUP, 0, 0, tiled=True)
    accel, residual, flag = call(
        last_kernel,
        [((3, NODES), F32), ((3, NODES), F32), ((1, 1), jnp.int32)],
        message, image, diag, inverse, *bases,
        smem_out=2,
    )

    def again(carry):
        args = same(load, element_mats, connect, shared)
        return (jnp.int32(1),) + tuple(same(*plain(*args)))

    _, accel, residual = lax.while_loop(lambda carry: carry[0] == 0, again, (flag.reshape(()), accel, residual))
    return accel, residual


def solution(mesh):
    parts = Mesh(mesh.devices.reshape(4, 16, 4, 2), AXES)
    return jax.shard_map(
        body,
        mesh=parts,
        in_specs=(P(None, AXES), P(None, None, AXES), P(None, AXES), P(None, AXES)),
        out_specs=(P(None, AXES), P(None, AXES)),
        check_vma=False,
    )
```

```python
import jax
import jax.numpy as jnp
from jax import lax
from jax.experimental import pallas as pl
from jax.experimental.pallas import tpu as pltpu
from jax.sharding import Mesh, PartitionSpec as P

ITERS = 4
AXES = ("x", "z", "y", "c")
GROUP = ("x", "y", "c")
NODES = 2048
ELEMS = 2048
SHARED = 256
SPLITS = 3
PIVOT_FLOOR = 0.02
F32 = jnp.float32
BF16 = jnp.bfloat16
EARLY_WORK = pl.CostEstimate(flops=2_000_000, bytes_accessed=400_000, transcendentals=0)
VMEM_LIMIT = 32 * 1024 * 1024


def iota(shape, dim):
    return lax.broadcasted_iota(jnp.int32, shape, dim)


def lane_take(table, lanes):
    return jnp.take_along_axis(table, lanes, axis=1, mode="promise_in_bounds")


def pick(parts, high):
    bit = 0
    while len(parts) > 1:
        odd = (high & (1 << bit)) != 0
        parts = [jnp.where(odd, parts[i + 1], parts[i]) for i in range(0, len(parts), 2)]
        bit += 1
    return parts[0]


def field_rows(field, block):
    return [jnp.broadcast_to(field[c * 16 + block : c * 16 + block + 1, :], (8, 128)) for c in range(3)]


def by_component(rows, comp):
    return jnp.where(comp == 0, rows[0], jnp.where(comp == 1, rows[1], rows[2]))


def halos_of(field, lists):
    comp = iota((8, 128), 0) // 2
    tables = [by_component(field_rows(field, block), comp) for block in range(16)]
    out = []
    for nodes in lists:
        out.append(pick([lane_take(t, nodes & 127) for t in tables], nodes >> 7))
    return out


def assembled(field, inverse, near, blocks=range(4)):
    tiles = []
    for c in range(3):
        for half in range(2):
            place = inverse[half * 8 : half * 8 + 8, :]
            lanes, code = place & 127, place >> 7
            parts = []
            for t in blocks:
                row = 2 * c + (t & 1)
                table = jnp.broadcast_to(near[t >> 1][row : row + 1, :], (8, 128))
                parts.append(lane_take(table, lanes))
            start = c * 16 + half * 8
            here = (code >= blocks[0]) & (code <= blocks[-1])
            tiles.append(field[start : start + 8, :] + jnp.where(here, pick(parts, code), 0.0))
    return jnp.concatenate(tiles, axis=0)


def bf16_rows(row, count):
    return jnp.broadcast_to(row.astype(F32), (count, row.shape[1])).astype(BF16)


def bf16_iota(shape):
    return iota(shape, 0).astype(F32).astype(BF16)


def high_mask(nodes):
    return bf16_rows(nodes >> 7, 16) == bf16_iota((16, nodes.shape[1]))


def corner_lhs(values, conn):
    zero = jnp.zeros((), BF16)
    parts = []
    rest = values
    for _ in range(SPLITS - 1):
        top = rest.astype(BF16).astype(F32)
        parts.append(top)
        rest = rest - top
    parts.append(rest)
    out = []
    for n in range(4):
        mask = high_mask(conn[n : n + 1, :])
        rows = [part[3 * n + c : 3 * n + c + 1, :] for part in parts for c in range(3)]
        out.append(jnp.concatenate([jnp.where(mask, bf16_rows(row, 16), zero) for row in rows], axis=0))
    return out


def times_one_hot(lhs, nodes):
    shape = (128, nodes.shape[1])
    hot = jnp.where(bf16_rows(nodes & 127, 128) == bf16_iota(shape), jnp.ones((), BF16), jnp.zeros((), BF16))
    return lax.dot_general(lhs, hot, (((1,), (1,)), ((), ())), preferred_element_type=F32)


def scatter(values_of, conn_ref):
    total = None
    for block in range(ELEMS // 256):
        start = block * 256
        conn = conn_ref[:, start : start + 256]
        lhs = corner_lhs(values_of(start), conn)
        for n in range(4):
            piece = times_one_hot(lhs[n], conn[n : n + 1, :])
            total = piece if total is None else total + piece
    out = total[0:48]
    for t in range(1, SPLITS):
        out = out + total[48 * t : 48 * t + 48]
    return out


def first_kernel(
    load_hbm, mats_hbm, conn_hbm, shared_hbm,
    load_out, lumped_out, mats_ref, conn_ref, lists_out, a_out, b_out,
    load_ref, shared_ref, sems,
):
    small = [
        pltpu.make_async_copy(shared_hbm, shared_ref, sems.at[0]),
        pltpu.make_async_copy(conn_hbm, conn_ref, sems.at[1]),
        pltpu.make_async_copy(load_hbm, load_ref, sems.at[2]),
    ]
    large = [
        pltpu.make_async_copy(mats_hbm.at[pl.ds(3 * i, 3)], mats_ref.at[pl.ds(3 * i, 3)], sems.at[3 + i]) for i in range(4)
    ]
    for copy in small[:2] + large + small[2:]:
        copy.start()
    for copy in small + large:
        copy.wait()
    odd = lax.axis_index("c") == 1
    own = shared_ref[...]
    row0, row1 = own[0:1, :], own[1:2, :]
    side_a = jnp.where(odd, row0, row1)
    side_b = jnp.where(odd, row1, row0)

    sub8 = iota((8, 128), 0)
    lists = []
    for side in (side_a, side_b):
        first = jnp.broadcast_to(side[:, 0:128], (8, 128))
        second = jnp.broadcast_to(side[:, 128:256], (8, 128))
        lists.append(jnp.where((sub8 & 1) == 0, first, second))
    lists_out[0:8, :] = lists[0]
    lists_out[8:16, :] = lists[1]

    for c in range(3):
        for h in range(16):
            load_out[c * 16 + h : c * 16 + h + 1, :] = load_ref[c : c + 1, h * 128 : h * 128 + 128]
    load_a, load_b = halos_of(load_out[...], lists)
    a_out[0:8, :] = load_a
    b_out[0:8, :] = load_b

    row12 = iota((12, 256), 0)
    zero16 = jnp.zeros((), BF16)
    lumped = None
    for block in range(ELEMS // 256):
        for n in range(4):
            span = slice(block * 256, block * 256 + 256)
            nodes = conn_ref[n : n + 1, span]
            mask = high_mask(nodes)
            rows = []
            for j in range(3 * n, 3 * n + 3):
                column = mats_ref[j, :, span].astype(F32)
                rows.append(jnp.where(mask, bf16_rows(column[j : j + 1, :], 16), zero16))
                mats_ref[j, :, span] = jnp.where(row12 == j, 0.0, column).astype(BF16)
            low = jnp.where(bf16_rows(nodes & 127, 128) == bf16_iota((128, 256)), jnp.ones((), BF16), zero16)
            piece = lax.dot_general(low, jnp.concatenate(rows, axis=0), (((1,), (1,)), ((), ())), preferred_element_type=F32)
            lumped = piece if lumped is None else lumped + piece
    lumped = lumped.T
    lumped_out[...] = lumped
    lump_a, lump_b = halos_of(lumped, lists)
    a_out[8:16, :] = lump_a
    b_out[8:16, :] = lump_b


def at_corners(tables_of, index_ref, out_ref):
    for t in range(2):
        tables = tables_of(t)
        for start in range(0, ELEMS, 128):
            nodes = index_ref[8 * t : 8 * t + 8, start : start + 128]
            lanes = nodes & 127
            out_ref[8 * t : 8 * t + 8, start : start + 128] = pick([lane_take(table, lanes) for table in tables], nodes >> 7)


def component_of_row(t):
    return (iota((8, 128), 0) + 2 * t) % 3


def corner_tables(field):
    rows = [field_rows(field, block) for block in range(16)]
    return lambda t: [by_component(r, component_of_row(t)) for r in rows]


def list_kernel(conn_ref, lists_ref, index_out, inverse_out, place_out):
    lane = iota((16, 256), 1)
    zero = jnp.zeros((), BF16)
    found = None
    for t in range(2):
        side = jnp.concatenate([lists_ref[8 * t : 8 * t + 1, :], lists_ref[8 * t + 1 : 8 * t + 2, :]], axis=1)
        mask = high_mask(side)
        place = jnp.where(mask, (lane & 127).astype(F32).astype(BF16), zero)
        code = jnp.where(mask, (2 * t + (lane >> 7) + 1).astype(F32).astype(BF16), zero)
        piece = times_one_hot(jnp.concatenate([place, code], axis=0), side)
        found = piece if found is None else found + piece
    inverse = (found[16:32].astype(jnp.int32) - 1) * 128 + found[0:16].astype(jnp.int32)
    inverse_out[...] = inverse
    for j in range(12):
        index_out[j : j + 1, :] = conn_ref[j // 3 : j // 3 + 1, :]
    index_out[12:16, :] = jnp.zeros((4, ELEMS), jnp.int32)
    tables = [jnp.broadcast_to(inverse[block : block + 1, :], (8, 128)) for block in range(16)]
    at_corners(lambda t: tables, index_out, place_out)


def early_kernel(past_ref, index_ref, *rest):
    if len(rest) == 3:
        diag_ref, corner_out, scale_out = rest
        at_corners(corner_tables(1.0 / diag_ref[...]), index_ref, scale_out)
    else:
        (corner_out,) = rest
    at_corners(corner_tables(past_ref[...]), index_ref, corner_out)


def apply_off_diagonal(corner, mats_ref, conn_ref):
    def product(start):
        gathered = corner(start)
        out = jnp.zeros((12, 128), F32)
        for j in range(12):
            column = mats_ref[j, :, start : start + 128].astype(F32)
            value = gathered[j // 8][j % 8 : j % 8 + 1, :]
            out = out + column * jnp.broadcast_to(value, (12, 128))
        return out

    def values_of(start):
        return jnp.concatenate([product(start), product(start + 128)], axis=1)

    return scatter(values_of, conn_ref)


def full_corner(field, index_ref, table_ref):
    of = corner_tables(field)
    for t in range(2):
        for block, table in enumerate(of(t)):
            table_ref[block, 8 * t : 8 * t + 8, :] = table

    def corner(start):
        index = index_ref[:, start : start + 128]
        gathered = []
        for t in range(2):
            nodes = index[8 * t : 8 * t + 8]
            lanes = nodes & 127
            gathered.append(pick([lane_take(table_ref[block, 8 * t : 8 * t + 8, :], lanes) for block in range(16)], nodes >> 7))
        return gathered

    return corner


def late_corner(corner_ref, scale_ref, place_ref, near):
    tables = []
    for t in range(2):
        comp = component_of_row(t)
        tables.append([])
        for block in range(4):
            k, values = block & 1, near[block >> 1]
            rows = [jnp.broadcast_to(values[2 * c + k : 2 * c + k + 1, :], (8, 128)) for c in range(3)]
            tables[t].append(by_component(rows, comp))

    def corner(start):
        gathered = []
        for t in range(2):
            at = (slice(8 * t, 8 * t + 8), slice(start, start + 128))
            place = place_ref[at]
            lanes, code = place & 127, place >> 7
            extra = pick([lane_take(table, lanes) for table in tables[t]], code)
            gathered.append((corner_ref[at] + jnp.where(code >= 0, extra, 0.0)) * scale_ref[at])
        return gathered

    return corner


def tile_sum(product):
    out = product[0:8, :]
    for i in range(1, 6):
        out = out + product[8 * i : 8 * i + 8, :]
    return out


def step(basis, corner, lumped_ref, mats_ref, conn_ref, lists_ref, image_out, sums_out):
    image = apply_off_diagonal(corner, mats_ref, conn_ref)
    image_out[...] = image
    sums_out[0:8, :] = tile_sum(basis * basis * lumped_ref[...])
    sums_out[8:16, :] = tile_sum(basis * image)
    return halos_of(image, [lists_ref[0:8, :], lists_ref[8:16, :]])


def second_kernel(
    load_ref, lumped_ref, inverse_ref, lists_ref, index_ref, conn_ref, mats_ref, near_b, near_a,
    diag_out, basis_out, image_out, sums_out, a_out, b_out, table_ref,
):
    inverse = inverse_ref[...]
    force = assembled(load_ref[...], inverse, [near_a[0:8, :], near_b[0:8, :]])
    diag = assembled(lumped_ref[...], inverse, [near_a[8:16, :], near_b[8:16, :]])
    basis = force / diag
    diag_out[...] = diag
    basis_out[...] = basis
    corner = full_corner(basis, index_ref, table_ref)
    halos = step(basis, corner, lumped_ref, mats_ref, conn_ref, lists_ref, image_out, sums_out)
    a_out[...] = halos[0]
    b_out[...] = halos[1]


def late_step(past_ref, corner_ref, scale_ref, place_ref, diag_ref, lumped_ref, inverse_ref, lists_ref, conn_ref, mats_ref, near_b, near_a, basis_out, image_out, sums_out):
    near = [near_a[...], near_b[...]]
    basis = assembled(past_ref[...], inverse_ref[...], near) / diag_ref[...]
    basis_out[...] = basis
    corner = late_corner(corner_ref, scale_ref, place_ref, near)
    return step(basis, corner, lumped_ref, mats_ref, conn_ref, lists_ref, image_out, sums_out)


def middle_kernel(
    past_ref, corner_ref, scale_ref, place_ref, diag_ref, lumped_ref, inverse_ref, lists_ref, conn_ref, mats_ref, near_b, near_a,
    basis_out, image_out, sums_out, a_out, b_out,
):
    halos = late_step(
        past_ref, corner_ref, scale_ref, place_ref, diag_ref, lumped_ref, inverse_ref, lists_ref, conn_ref, mats_ref, near_b, near_a,
        basis_out, image_out, sums_out,
    )
    a_out[...] = halos[0]
    b_out[...] = halos[1]


def place():
    return tuple(lax.axis_index(a) for a in AXES)


def slab_slot(slab):
    return (slab // 128) * 8 + slab % 8


def fourth_kernel(
    past_ref, corner_ref, scale_ref, place_ref, diag_ref, lumped_ref, inverse_ref, lists_ref, conn_ref, mats_ref, near_b, near_a,
    sums0, sums1, sums2,
    basis_out, image_out, message_out, sums_ref,
):
    halos = late_step(
        past_ref, corner_ref, scale_ref, place_ref, diag_ref, lumped_ref, inverse_ref, lists_ref, conn_ref, mats_ref, near_b, near_a,
        basis_out, image_out, sums_ref,
    )
    lane = iota((8, 128), 1)
    sub = iota((8, 128), 0)
    moments = jnp.zeros((8, 128), F32)
    for k, ref in enumerate((sums0, sums1, sums2, sums_ref)):
        for t in range(2):
            total = jnp.sum(ref[8 * t : 8 * t + 8, :], axis=0, keepdims=True)
            total = jnp.sum(jnp.broadcast_to(total, (8, 128)), axis=1, keepdims=True)
            moments = jnp.where(lane == 2 * k + t, total, moments)
    moments = jnp.where(sub == 6, moments, 0.0)
    message_out[...] = jnp.broadcast_to(moments[None], (32, 8, 128))
    x, z, y, c = place()
    slab = ((x * 16 + z) * 4 + y) * 2 + c
    odd = c == 1
    to_right = jnp.where(sub < 6, jnp.where(odd, halos[1], halos[0]), moments)
    to_left = jnp.where(sub < 6, jnp.where(odd, halos[0], halos[1]), moments)

    @pl.when(slab < 511)
    def _():
        message_out[slab_slot(jnp.minimum(slab + 1, 511))] = to_right

    @pl.when(slab > 0)
    def _():
        message_out[slab_slot(jnp.maximum(slab - 1, 0))] = to_left


def relay_kernel(message_ref, message_out, direct_out):
    x, z, y, c = place()
    slot = x * 8 + y * 2 + c
    first = (y == 0) & (c == 0)
    last = (y == 3) & (c == 1)
    sub = iota((8, 128), 0)
    moments = message_ref[0]
    for i in range(1, 32):
        moments = moments + message_ref[i]
    moments = jnp.where(sub == 6, moments, 0.0)
    message_out[...] = jnp.broadcast_to(moments[None], (16, 8, 128))
    source_r = jnp.where(first, jnp.where(z < 15, x * 8 + 7, jnp.maximum(x * 8 - 1, 0)), jnp.maximum(slot - 1, 0))
    source_l = jnp.where(last, jnp.where(z > 0, x * 8, jnp.minimum(x * 8 + 8, 31)), jnp.minimum(slot + 1, 31))
    from_left = message_ref[source_r]
    from_right = message_ref[source_l]
    direct_out[0:8, :] = from_left
    direct_out[8:16, :] = from_right

    @pl.when(first)
    def _():
        message_out[(z + 1) % 16] = jnp.where(sub < 6, from_left, moments)

    @pl.when(last)
    def _():
        message_out[(z + 15) % 16] = jnp.where(sub < 6, from_right, moments)


def coefficients(moment):
    zero, one = jnp.zeros((8, 128), F32), jnp.ones((8, 128), F32)
    scale = [jnp.where(moment[2 * i] > 0.0, lax.rsqrt(jnp.where(moment[2 * i] > 0.0, moment[2 * i], one)), zero) for i in range(4)]
    rows = [[moment[i + j] * scale[i] * scale[j] for j in range(4)] + [-moment[i + 4] * scale[i]] for i in range(4)]
    least = one
    inverse = []
    for i in range(4):
        pivot = rows[i][i]
        good = pivot > 1e-6
        least = jnp.minimum(least, jnp.where(good, pivot, zero))
        inverse.append(jnp.where(good, one / jnp.where(good, pivot, one), zero))
        for j in range(i + 1, 4):
            ratio = rows[j][i] * inverse[i]
            for k in range(i + 1, 5):
                rows[j][k] = rows[j][k] - ratio * rows[i][k]
    coef = [zero] * 4
    for i in (3, 2, 1, 0):
        total = rows[i][4]
        for j in range(i + 1, 4):
            total = total - rows[i][j] * coef[j]
        coef[i] = total * inverse[i]
    coef = [coef[i] * scale[i] for i in range(4)]
    at = coef[0] - coef[1] + coef[2] - coef[3] + one
    resid = [v / at for v in coef] + [one / at]
    accel = [None] * 4
    accel[3] = -resid[4]
    for i in (2, 1, 0):
        accel[i] = -resid[i + 1] - accel[i + 1]
    good = (least > PIVOT_FLOOR) & (at > 0.0)
    return accel, resid, good


def last_kernel(message_ref, direct_ref, image_ref, diag_ref, inverse_ref, b0, b1, b2, b3, accel_out, resid_out, flag_out):
    x, z, y, c = place()
    slab = ((x * 16 + z) * 4 + y) * 2 + c
    first = (y == 0) & (c == 0)
    last = (y == 3) & (c == 1)
    lane = iota((8, 128), 1)
    total = message_ref[0]
    for i in range(1, 16):
        total = total + message_ref[i]
    total = jnp.broadcast_to(total[6:7, :], (8, 128))
    moment = [
        jnp.broadcast_to(jnp.sum(jnp.where(lane == k, total, 0.0), axis=1, keepdims=True), (8, 128)) for k in range(8)
    ]
    accel_coef, resid_coef, good = coefficients(moment)
    from_left = jnp.where(first, message_ref[(z + 15) % 16], direct_ref[0:8, :])
    from_right = jnp.where(last, message_ref[(z + 1) % 16], direct_ref[8:16, :])
    from_left = jnp.where(slab > 0, from_left, 0.0)
    from_right = jnp.where(slab < 511, from_right, 0.0)
    odd = c == 1
    near = [jnp.where(odd, from_left, from_right), jnp.where(odd, from_right, from_left)]
    diag = diag_ref[...]
    image = assembled(image_ref[...], inverse_ref[...], near)
    for c_ in range(3):
        for half in range(2):
            rows = slice(c_ * 16 + half * 8, c_ * 16 + half * 8 + 8)
            basis = [r[rows, :] for r in (b0, b1, b2, b3)]
            accel = basis[3] * accel_coef[3]
            part = basis[3] * resid_coef[3]
            for k in (2, 1, 0):
                accel = accel + basis[k] * accel_coef[k]
                part = part + basis[k] * resid_coef[k]
            resid = image[rows, :] * resid_coef[4] + diag[rows, :] * part
            for h in range(8):
                start = (half * 8 + h) * 128
                accel_out[c_ : c_ + 1, start : start + 128] = accel[h : h + 1, :]
                resid_out[c_ : c_ + 1, start : start + 128] = resid[h : h + 1, :]
    flag_out[0, 0] = jnp.min(jnp.where(good, 1, 0))


def call(kernel, outs, *args, scratch=(), smem_out=None, space=pltpu.VMEM, work=None):
    out_specs = [pl.BlockSpec(memory_space=pltpu.VMEM)] * len(outs)
    if smem_out is not None:
        out_specs[smem_out] = pl.BlockSpec(memory_space=pltpu.SMEM)
    return pl.pallas_call(
        kernel,
        out_shape=[jax.ShapeDtypeStruct(s, t) for s, t in outs],
        in_specs=[pl.BlockSpec(memory_space=space)] * len(args),
        out_specs=out_specs,
        scratch_shapes=list(scratch),
        compiler_params=pltpu.CompilerParams(vmem_limit_bytes=VMEM_LIMIT),
        cost_estimate=work,
    )(*args)


def same(*args):
    def kernel(*refs):
        for src, dst in zip(refs[: len(args)], refs[len(args) :]):
            dst[...] = src[...]

    return call(kernel, [(a.shape, a.dtype) for a in args], *args)


def swap(side_a, side_b):
    count = 512
    from_b = lax.ppermute(side_b, AXES, [(i, ((i + 1) ^ 1) - 1) for i in range(1, count - 1)])
    from_a = lax.ppermute(side_a, AXES, [(i, i ^ 1) for i in range(count)])
    return from_a, from_b


def plain(load, element_mats, connect, shared):
    node_count = load.shape[1]
    slab_index = lax.axis_index(AXES)
    slab_count = 512
    left_weight = jnp.where(slab_index > 0, F32(0.5), F32(1.0))
    right_weight = jnp.where(slab_index < slab_count - 1, F32(0.5), F32(1.0))
    weights = jnp.ones((node_count,), F32).at[shared[0]].set(left_weight).at[shared[1]].set(right_weight)

    def inner(first, second):
        return lax.psum(jnp.sum(weights * jnp.sum(first * second, axis=0)), AXES)

    def assemble(partial_value):
        from_left = lax.ppermute(partial_value[:, shared[1]], AXES, [(i, i + 1) for i in range(slab_count - 1)])
        from_right = lax.ppermute(partial_value[:, shared[0]], AXES, [(i + 1, i) for i in range(slab_count - 1)])
        return partial_value.at[:, shared[0]].add(from_left).at[:, shared[1]].add(from_right)

    def spread(values):
        values = values.reshape(4, 3, -1).transpose(1, 0, 2).reshape(3, -1)
        return jnp.zeros((3, node_count), F32).at[:, connect.reshape(-1)].add(values)

    def element_apply(field):
        gathered = field[:, connect].transpose(1, 0, 2).reshape(12, -1)
        result = element_mats[:, 0, :].astype(F32) * gathered[0]
        for column in range(1, 12):
            result = result + element_mats[:, column, :].astype(F32) * gathered[column]
        return spread(result)

    lumped = spread(jnp.stack([element_mats[i, i, :].astype(F32) for i in range(12)]))
    both = assemble(jnp.concatenate([load, lumped], axis=0))
    residual, diagonal = both[:3], both[3:]
    direction = residual / diagonal
    accel = jnp.zeros_like(residual)
    gamma = inner(residual, direction)

    def body(_, carry):
        accel, residual, direction, gamma = carry
        image = assemble(element_apply(direction))
        alpha = gamma / inner(direction, image)
        accel = accel + alpha * direction
        residual = residual - alpha * image
        precond = residual / diagonal
        following = inner(residual, precond)
        return accel, residual, precond + following / gamma * direction, following

    accel, residual, _, _ = lax.fori_loop(0, ITERS, body, (accel, residual, direction, gamma))
    return accel, residual


def body(load, element_mats, connect, shared):
    field = ((48, 128), F32)
    halo = ((8, 128), F32)
    sums = ((16, 128), F32)
    corners = ((16, ELEMS), F32)
    index = ((16, ELEMS), jnp.int32)
    inverse = ((16, 128), jnp.int32)
    load_f, lumped, mats, conn, lists, a, b = call(
        first_kernel,
        [field, field, ((12, 12, ELEMS), BF16), ((4, ELEMS), jnp.int32), inverse, sums, sums],
        load, element_mats, connect, shared,
        scratch=[pltpu.VMEM((3, NODES), F32), pltpu.VMEM((2, SHARED), jnp.int32), pltpu.SemaphoreType.DMA((7,))],
        space=pltpu.HBM,
    )
    a, b = swap(a, b)
    index, inverse, places = call(list_kernel, [index, inverse, index], conn, lists, work=EARLY_WORK)
    diag, b0, image, total, a, b = call(
        second_kernel,
        [field, field, field, sums, halo, halo],
        load_f, lumped, inverse, lists, index, conn, mats, b, a,
        scratch=[pltpu.VMEM((16, 16, 128), F32)],
    )
    bases, totals = [b0], [total]
    for round_ in range(3):
        a, b = swap(a, b)
        if round_ == 0:
            corner, scale = call(early_kernel, [corners, corners], image, index, diag, work=EARLY_WORK)
        else:
            (corner,) = call(early_kernel, [corners], image, index, work=EARLY_WORK)
        args = (image, corner, scale, places, diag, lumped, inverse, lists, conn, mats, b, a)
        if round_ < 2:
            basis, image, total, a, b = call(middle_kernel, [field, field, sums, halo, halo], *args)
            bases.append(basis)
            totals.append(total)
    basis, image, message = call(
        fourth_kernel,
        [field, field, ((32, 8, 128), F32)],
        *args, *totals,
        scratch=[pltpu.VMEM((16, 128), F32)],
    )
    bases.append(basis)
    message = lax.all_to_all(message, GROUP, 0, 0, tiled=True)
    message, direct = call(relay_kernel, [((16, 8, 128), F32), sums], message)
    message = lax.all_to_all(message, "z", 0, 0, tiled=True)
    accel, residual, flag = call(
        last_kernel,
        [((3, NODES), F32), ((3, NODES), F32), ((1, 1), jnp.int32)],
        message, direct, image, diag, inverse, *bases,
        smem_out=2,
    )

    def again(carry):
        args = same(load, element_mats, connect, shared)
        return (jnp.int32(1),) + tuple(same(*plain(*args)))

    _, accel, residual = lax.while_loop(lambda carry: carry[0] == 0, again, (flag.reshape(()), accel, residual))
    return accel, residual


def solution(mesh):
    parts = Mesh(mesh.devices.reshape(4, 16, 4, 2), AXES)
    return jax.shard_map(
        body,
        mesh=parts,
        in_specs=(P(None, AXES), P(None, None, AXES), P(None, AXES), P(None, AXES)),
        out_specs=(P(None, AXES), P(None, AXES)),
        check_vma=False,
    )
```
